512 devices in a mesh: gx: 8 (over x, core), gy: 8 (over z_lo), gz: 8 (over y, z_hi).
Axes of the slice: x: 4, y: 4, z: 16 (z_hi: 2, z_lo: 8; z = z_hi * 8 + z_lo), core: 2. Of those that a mesh axis runs over, the one named last changes fastest.
Arguments:
- hidden: bfloat16 [1024, 26624], P(('gz', 'gy'), 'gx'), may hold values from -16 to 16
- out_grad: bfloat16 [1024, 16384], P(('gz', 'gx'), 'gy'), may hold values from -16 to 16
- weight: bfloat16 [26624, 16384], P('gx', ('gy', 'gz')), may hold values from -0.0390625 to 0.0390625
- adapter_down_factor: bfloat16 [26624, 16], P('gx'), may hold values from -0.109375 to 0.109375
- adapter_up_factor: bfloat16 [16, 16384], P(None, 'gy'), may hold values from -0.125 to 0.125
Outputs:
- hidden_gradient: bfloat16 [1024, 26624], P(('gz', 'gy'), 'gx')
- recomputed: bfloat16 [1024, 16384], P(('gz', 'gx'), 'gy')
- grad_down: float32 [26624, 16], P(('gx', 'gz'))
- grad_up: float32 [16, 16384], P(None, ('gy', 'gz'))
The draws below stay inside these ranges and needn't reach their ends.
All inputs are finite; a program needn't handle non-finite values.
Results may differ from the reference program's by a relative error of at most 0.017.
Values may be sent and summed in bfloat16 or wider, within the bound.
A program may use at most 64 MiB of HBM per device.

```python
import jax
import jax.numpy as jnp
from jax import lax

D = 16384
FF = 26624
RANK = 16
TOKEN_COUNT = 1024
N_GX = 8
N_GY = 8


def with_spikes(array, key, source, target, parts, factor):
    def block_of(position):
        return (jnp.arange(array.shape[position]) // (array.shape[position] // parts)).reshape((-1,) + (1,) * (array.ndim - 1 - position))

    one_side = jax.random.permutation(key, parts)[block_of(target)]
    far = (block_of(target) + parts // 2) % parts
    return jnp.where((block_of(source) == one_side) | (block_of(source) == far), factor * array, array)


def steps_of(key, dims, pieces, least, largest):
    loudness, own = 1.0, jax.random.fold_in(key, 6)
    for axis_at, parts in pieces:
        draws = jnp.exp(jax.random.uniform(jax.random.fold_in(own, axis_at), (parts,), jnp.float32, least / len(pieces), largest / len(pieces)))
        loudness = loudness * jnp.repeat(draws, dims[axis_at] // parts).reshape([-1 if axis == axis_at else 1 for axis in range(len(dims))])
    return loudness


def centred(key, extent, width, most, pieces=(), kind=jnp.bfloat16):
    array = jax.random.normal(key, extent, jnp.float32) * width
    if len(pieces) > 0:
        array = steps_of(key, extent, pieces, -0.22, 0.18) * array
    return jnp.clip(array, min=-most, max=most).astype(kind)


def heavy_noise(rng, shape, deviation, limit, cuts, heavy, dtype=jnp.bfloat16):
    values = deviation * jax.random.normal(rng, shape, jnp.float32)
    if cuts:
        values = values * steps_of(rng, shape, cuts, -0.22, 0.18)
    return jnp.clip(with_spikes(values, jax.random.fold_in(rng, 3), *heavy), -limit, limit).astype(dtype)


def setup_inputs(seed: int = 0) -> dict:
    splits = jax.random.split(jax.random.key(seed), 6)
    return {
        "hidden": heavy_noise(splits[0], (TOKEN_COUNT, FF), 1.0, 16.0, ((0, 64), (1, 8)), (0, 1, 64, 4.0)),
        "out_grad": heavy_noise(splits[1], (TOKEN_COUNT, D), 1.0, 16.0, ((0, 64), (1, 8)), (0, 1, 64, 4.0)),
        "weight": centred(splits[2], (FF, D), FF ** -0.5, 0.0390625, ((0, 8), (1, 64))),
        "adapter_down_factor": centred(splits[3], (FF, RANK), (FF // 8) ** -0.5, 0.109375, ((0, 8),)),
        "adapter_up_factor": centred(splits[4], (RANK, D), (D // 8) ** -0.5, 0.125, ((1, 8),)),
    }


adapter_scale = 2.0


def settle(value):
    return lax.optimization_barrier(value.astype(jnp.bfloat16)).astype(jnp.float32)


def reference(hidden, out_grad, weight, adapter_down_factor, adapter_up_factor):
    down_lowrank = jnp.dot(out_grad, adapter_up_factor.T, preferred_element_type=jnp.float32).astype(jnp.bfloat16)
    up_lowrank = jnp.dot(hidden, adapter_down_factor, preferred_element_type=jnp.float32).astype(jnp.bfloat16)
    feature_cut = D // N_GY
    input_frozen_part = jnp.zeros((TOKEN_COUNT, FF), jnp.float32)
    for column_block in range(N_GY):
        lower = column_block * feature_cut
        partial_value = jnp.dot(out_grad[:, lower:lower + feature_cut], weight[:, lower:lower + feature_cut].T, preferred_element_type=jnp.float32)
        input_frozen_part = input_frozen_part + settle(partial_value)
    hidden_gradient = (input_frozen_part + adapter_scale * jnp.dot(down_lowrank, adapter_down_factor.T, preferred_element_type=jnp.float32)).astype(jnp.bfloat16)
    unit_cut = FF // N_GX
    output_frozen_part = jnp.zeros((TOKEN_COUNT, D), jnp.float32)
    for row_block in range(N_GX):
        lower = row_block * unit_cut
        partial_value = jnp.dot(hidden[:, lower:lower + unit_cut], weight[lower:lower + unit_cut, :], preferred_element_type=jnp.float32)
        output_frozen_part = output_frozen_part + settle(partial_value)
    recomputed = (output_frozen_part + adapter_scale * jnp.dot(up_lowrank, adapter_up_factor, preferred_element_type=jnp.float32)).astype(jnp.bfloat16)
    factor_matrix = adapter_scale / TOKEN_COUNT
    grad_down = jnp.dot(hidden.T, down_lowrank, preferred_element_type=jnp.float32) * factor_matrix
    grad_up = jnp.dot(up_lowrank.T, out_grad, preferred_element_type=jnp.float32) * factor_matrix
    return hidden_gradient, recomputed, grad_down, grad_up
```

```python
import functools

import jax
import jax.numpy as jnp
from jax import lax
from jax.experimental import pallas as pl
from jax.experimental.pallas import tpu as pltpu
from jax.sharding import PartitionSpec as P

MESH = pl.DeviceIdType.MESH
BF = jnp.bfloat16
F32 = jnp.float32

FF = 3328
UNIT = 256
UNITS = FF // UNIT
HALF = UNIT // 2
TOK = 256
FEAT = 1024
AHEAD = 3
WIN = 512


def nt(left, right):
    return lax.dot_general(left, right, (((1,), (1,)), ((), ())), preferred_element_type=F32)


def nn(left, right):
    return jnp.dot(left, right, preferred_element_type=F32)


def mod(value, size):
    return lax.rem(value + size, size)


def rows16(block):
    return pl.ds(pl.multiple_of(block * 16, 16), 16)


def unit_cols(unit):
    return pl.ds(pl.multiple_of(unit * UNIT, UNIT), UNIT)


def kernel(
    hid, og, w, ad, au,
    hg, rec, gd, gu,
    W, H, G, I, O, Ob, plus, minus, AD, ADT, AU, PD, PU, DT, UT, GDs, GDr, GUs, GUr, OX, OPs, OPr,
    lsem, wds, wdr, wfs, wfr, hs, hr, gzs, gzr, gxs, gxr, pds, pdr, pus, pur, gys, gyr,
    rps, rpr, rms, rmr, oxs, oxr, ops_, opr,
):
    gx, gy, gz = lax.axis_index("gx"), lax.axis_index("gy"), lax.axis_index("gz")
    y, zh = lax.div(gz, 2), lax.rem(gz, 2)
    z = zh * 8 + gy

    def zdev(where):
        return {"gy": lax.rem(where, 8), "gz": y * 2 + lax.div(where, 8)}

    def ydev(where):
        return {"gz": where * 2 + zh}

    zup, zdown = zdev(mod(z + 1, 16)), zdev(mod(z - 1, 16))
    yup, ydown = mod(y + 1, 4), mod(y - 1, 4)
    yfar = mod(y + 2, 4)
    partner = {"gz": y * 2 + (1 - zh)}

    def remote(src, dst, ssem, rsem, to):
        return pltpu.make_async_remote_copy(
            src_ref=src, dst_ref=dst, send_sem=ssem, recv_sem=rsem, device_id=to, device_id_type=MESH
        )

    my_cols = pl.ds(pl.multiple_of(y * 256, 256), 256)

    def quarter(q, which):
        return pl.ds(pl.multiple_of((2 * q + which) * 256, 256), 256)

    mine = rows16(zh * 8 + gx)
    theirs = rows16((1 - zh) * 8 + gx)
    loads = [
        pltpu.make_async_copy(hid, H.at[rows16(z), :], lsem.at[0]),
        pltpu.make_async_copy(w, W.at[:, my_cols], lsem.at[1]),
        pltpu.make_async_copy(ad, AD, lsem.at[2]),
    ]
    for q in range(4):
        loads.append(pltpu.make_async_copy(og.at[:, quarter(q, zh)], G.at[mine, q * 256:(q + 1) * 256], lsem.at[3 + q]))
        loads.append(pltpu.make_async_copy(au.at[:, quarter(q, zh)], AU.at[:, q * 256:(q + 1) * 256], lsem.at[7 + q]))
    for load in loads:
        load.start()

    barrier = pltpu.get_barrier_semaphore()
    peers = [zup, zdown, partner, ydev(yup), ydev(ydown), ydev(yfar)]
    peers += [{"gx": mod(gx + i, 8)} for i in range(1, 8)]
    for peer in peers:
        pl.semaphore_signal(barrier, inc=1, device_id=peer, device_id_type=MESH)
    pl.semaphore_wait(barrier, len(peers))

    def w_rows(unit):
        return pl.ds(pl.multiple_of(unit * UNIT, UNIT), UNIT)

    def w_first(unit):
        return pl.ds(pl.multiple_of(unit * UNIT, HALF), HALF)

    def w_second(unit):
        return pl.ds(pl.multiple_of(unit * UNIT + HALF, HALF), HALF)

    def cols_of(where):
        return pl.ds(pl.multiple_of(where * 256, 256), 256)

    def w_direct(unit, side):
        return remote(
            w.at[w_rows(unit), :], W.at[w_rows(unit), my_cols], wds.at[side, unit], wdr.at[side, unit],
            ydev(yup if side == 0 else ydown),
        )

    def w_arrived(unit, side):
        part = W.at[w_rows(unit), cols_of(ydown if side == 0 else yup)]
        return remote(part, part, wds.at[side, unit], wdr.at[side, unit], ydev(yup))

    def w_pass(unit, side):
        part = W.at[w_first(unit) if side == 0 else w_second(unit), cols_of(ydown if side == 0 else yup)]
        return remote(part, part, wfs.at[side, unit], wfr.at[side, unit], ydev(yup if side == 0 else ydown))

    def w_passed(unit, side):
        part = W.at[w_first(unit) if side == 0 else w_second(unit), cols_of(yfar)]
        return remote(part, part, wfs.at[side, unit], wfr.at[side, unit], ydev(yup))

    def w_step(unit):
        @pl.when(unit + AHEAD < UNITS)
        def _():
            w_direct(unit + AHEAD, 0).start()
            w_direct(unit + AHEAD, 1).start()

        for side in range(2):
            w_arrived(unit, side).wait_recv()
            w_pass(unit, side).start()

    for unit in range(AHEAD):
        w_direct(unit, 0).start()
        w_direct(unit, 1).start()

    for q in range(4):
        remote(og.at[:, quarter(q, 1 - zh)], G.at[mine, q * 256:(q + 1) * 256], gzs, gzr, partner).start()

    def h_move(step, side):
        part = H.at[rows16(mod(z - step if side == 0 else z + step, 16)), :]
        return remote(part, part, hs.at[side, step], hr.at[side, step], zup if side == 0 else zdown)

    def h_got(step, side):
        part = H.at[rows16(mod(z - 1 - step if side == 0 else z + 1 + step, 16)), :]
        return remote(part, part, hs.at[side, step], hr.at[side, step], zup)

    def h_step(step):
        h_got(step, 0).wait_recv()
        if step < 7:
            h_move(step + 1, 0).start()
            h_got(step, 1).wait_recv()
        if step < 6:
            h_move(step + 1, 1).start()

    loads[0].wait()
    h_move(0, 0).start()
    h_move(0, 1).start()

    def g_send(i, rows, which):
        return remote(G.at[rows, :], G.at[rows, :], gxs.at[which], gxr.at[which], {"gx": mod(gx + i, 8)})

    for load in loads[3:]:
        load.wait()
    for i in range(1, 8):
        g_send(i, mine, 0).start()
    w_step(0)
    h_step(0)
    remote(G.at[theirs, :], G.at[theirs, :], gzs, gzr, partner).wait_recv()
    for i in range(1, 8):
        g_send(i, theirs, 1).start()
    h_step(1)
    w_step(1)
    h_step(2)
    h_step(3)
    w_step(2)
    h_step(4)
    loads[2].wait()
    eye = (lax.broadcasted_iota(jnp.int32, (16, 16), 0) == lax.broadcasted_iota(jnp.int32, (16, 16), 1)).astype(BF)

    def transpose_unit(unit, _):
        ADT[:, unit_cols(unit)] = nt(eye, AD[w_rows(unit), :]).astype(BF)
        return 0

    lax.fori_loop(0, UNITS, transpose_unit, 0)
    h_step(5)

    for which in range(2):
        part = G.at[0:112, :]
        remote(part, part, gxs.at[which], gxr.at[which], {"gx": mod(gx + 1, 8)}).wait_recv()
    PD[pl.ds(z, 1)] = nt(AU[...], G[...]).reshape(1, 16, TOK)

    def pd_move(step, side):
        part = PD.at[mod(z - step if side == 0 else z + step, 16)]
        return remote(part, part, pds.at[side, step], pdr.at[side, step], zup if side == 0 else zdown)

    def pd_got(step, side):
        part = PD.at[mod(z - 1 - step if side == 0 else z + 1 + step, 16)]
        return remote(part, part, pds.at[side, step], pdr.at[side, step], zup)

    pd_move(0, 0).start()
    pd_move(0, 1).start()
    w_step(3)
    h_step(6)
    h_step(7)

    def up_unit(unit, total):
        return total + nt(ADT[:, unit_cols(unit)], H[:, unit_cols(unit)])

    PU[pl.ds(gx, 1)] = lax.fori_loop(0, UNITS, up_unit, jnp.zeros((16, TOK), F32)).reshape(1, 16, TOK)

    def pu_send(i):
        return remote(PU.at[gx], PU.at[gx], pus.at[i - 1], pur.at[i - 1], {"gx": mod(gx + i, 8)})

    def pu_got(i):
        part = PU.at[mod(gx - i, 8)]
        return remote(part, part, pus.at[i - 1], pur.at[i - 1], {"gx": mod(gx + i, 8)})

    for i in range(1, 8):
        pu_send(i).start()

    O[...] = jnp.zeros_like(O)
    loads[1].wait()

    def compute(unit):
        for side in range(2):
            w_passed(unit, side).wait_recv()
        block = W[w_rows(unit), :]
        I[:, unit_cols(unit)] = nt(G[...], block).astype(BF)
        O[...] += nn(H[:, unit_cols(unit)], block)

    def pick(block):
        return (
            lax.broadcasted_iota(jnp.int32, (16, TOK), 1)
            == lax.broadcasted_iota(jnp.int32, (16, TOK), 0) + block * 16
        ).astype(BF)

    def ring_plus(k, unit):
        cols = unit_cols(unit)
        if k == 0:
            src = I.at[rows16(mod(z + 8, 16)), cols]
        else:
            part = plus.at[k - 1, :, cols]
            remote(part, part, rps.at[k - 1, unit], rpr.at[k - 1, unit], zup).wait_recv()
            plus[k - 1, :, cols] = (
                plus[k - 1, :, cols].astype(F32) + I[rows16(mod(z + 8 - k, 16)), cols].astype(F32)
            ).astype(BF)
            src = part
        remote(src, plus.at[k, :, cols], rps.at[k, unit], rpr.at[k, unit], zup).start()

    def ring_minus(k, unit):
        cols = unit_cols(unit)
        if k == 0:
            src = I.at[rows16(mod(z - 7, 16)), cols]
        else:
            part = minus.at[k - 1, :, cols]
            remote(part, part, rms.at[k - 1, unit], rmr.at[k - 1, unit], zdown).wait_recv()
            minus[k - 1, :, cols] = (
                minus[k - 1, :, cols].astype(F32) + I[rows16(mod(z - 7 + k, 16)), cols].astype(F32)
            ).astype(BF)
            src = part
        remote(src, minus.at[k, :, cols], rms.at[k, unit], rmr.at[k, unit], zdown).start()

    def ring_end(unit):
        cols = unit_cols(unit)
        up, down = plus.at[7, :, cols], minus.at[6, :, cols]
        remote(up, up, rps.at[7, unit], rpr.at[7, unit], zup).wait_recv()
        remote(down, down, rms.at[6, unit], rmr.at[6, unit], zdown).wait_recv()
        total = plus[7, :, cols].astype(F32) + minus[6, :, cols].astype(F32) + I[rows16(z), cols].astype(F32)
        low = nt(pick(z), DT[...]).astype(BF)
        hg[:, cols] = (total + 2.0 * nn(low, ADT[:, cols])).astype(BF)

    def window(where):
        block = 2 * where + zh
        return pl.ds(pl.multiple_of(lax.div(block * 13, 4) * 128, 128), WIN)

    def gy_send(kind, i):
        src, dst = (GDs.at[i], GDr.at[i - 1]) if kind == 0 else (GUs.at[i], GUr.at[i - 1])
        return remote(src, dst, gys.at[kind, i - 1], gyr.at[kind, i - 1], ydev(mod(y + i, 4)))

    def ox_rows(which):
        return rows16(which * 8 + gx)

    def ox_send(i, which):
        to = mod(gx + i, 8)
        return remote(
            Ob.at[rows16(which * 8 + to), :], OX.at[i, which], oxs, oxr, {"gx": to}
        )

    def loop(i, _):
        for at, unit in ((1, 4), (3, 5), (4, 6)):
            @pl.when(i == at)
            def _(unit=unit):
                w_step(jnp.int32(unit))

        @pl.when((i >= 6) & (i < 12))
        def _():
            w_step(i + 1)

        @pl.when(i < UNITS)
        def _():
            compute(i)

        for step in range(8):
            @pl.when(i == step)
            def _(step=step):
                pd_got(step, 0).wait_recv()
                if step < 7:
                    pd_move(step + 1, 0).start()
                    pd_got(step, 1).wait_recv()
                if step < 6:
                    pd_move(step + 1, 1).start()

        @pl.when(i == 3)
        def _():
            for j in range(1, 8):
                pu_got(j).wait_recv()
            UT[...] = jnp.sum(PU[...], axis=0).astype(BF)
            for j in range(4):
                cols = cols_of(mod(y + j, 4))
                GUs[j] = nn(UT[...], G[:, cols])
                if j:
                    gy_send(1, j).start()

        @pl.when(i == 7)
        def _():
            DT[...] = jnp.sum(PD[...], axis=0).astype(BF)
            for j in range(4):
                GDs[j] = nn(DT[...], H[:, window(mod(y + j, 4))])
                if j:
                    gy_send(0, j).start()

        @pl.when(i >= 8)
        def _():
            ring_end(i - 8)

        for k in range(7, -1, -1):
            @pl.when((i - k >= 0) & (i - k < UNITS))
            def _(k=k):
                ring_plus(k, i - k)
                if k < 7:
                    ring_minus(k, i - k)

        @pl.when(i == UNITS - 1)
        def _():
            Ob[...] = O[...].astype(BF)
            for j in range(1, 8):
                for which in range(2):
                    ox_send(j, which).start()

        @pl.when(i == UNITS + 4)
        def _():
            part = OX.at[1:8]
            remote(part, part, oxs, oxr, zup).wait_recv()
            for which, block in ((0, 1 - zh), (1, zh)):
                total = O[ox_rows(block), :]
                for j in range(1, 8):
                    total = total + OX[j, block].astype(F32)
                low = nt(pick(block * 8 + gx), UT[...]).astype(BF)
                result = (total + 2.0 * nn(low, AU[...])).astype(BF)
                if which == 0:
                    OPs[...] = result
                    remote(OPs, OPr, ops_, opr, partner).start()
                else:
                    for q in range(4):
                        rec[:, quarter(q, zh)] = result[:, q * 256:(q + 1) * 256]

        return 0

    lax.fori_loop(0, UNITS + 8, loop, 0)

    for j in range(1, 4):
        for kind in range(2):
            gy_send(kind, j).wait_recv()
    gd[...] = (GDs[0] + GDr[0] + GDr[1] + GDr[2]) * (2.0 / 1024)
    gu[...] = (GUs[0] + GUr[0] + GUr[1] + GUr[2]) * (2.0 / 1024)

    remote(OPs, OPr, ops_, opr, partner).wait_recv()
    for q in range(4):
        rec[:, quarter(q, 1 - zh)] = OPr[:, q * 256:(q + 1) * 256]

    remote(OPs, OPr, ops_, opr, partner).wait_send()
    part = OX.at[1:8]
    remote(part, part, oxs, oxr, zup).wait_send()
    remote(G.at[mine, :], G.at[mine, :], gzs, gzr, partner).wait_send()
    for which in range(2):
        remote(G.at[0:112, :], G.at[0:112, :], gxs.at[which], gxr.at[which], zup).wait_send()
    for j in range(1, 8):
        pu_send(j).wait_send()
    for j in range(1, 4):
        for kind in range(2):
            gy_send(kind, j).wait_send()
    for step in range(8):
        for side in range(2 if step < 7 else 1):
            h_move(step, side).wait_send()
            pd_move(step, side).wait_send()

    def finish(unit, _):
        for side in range(2):
            w_direct(unit, side).wait_send()
            w_pass(unit, side).wait_send()
        cols = unit_cols(unit)
        for k in range(8):
            remote(plus.at[k, :, cols], plus.at[k, :, cols], rps.at[k, unit], rpr.at[k, unit], zup).wait_send()
            if k < 7:
                remote(minus.at[k, :, cols], minus.at[k, :, cols], rms.at[k, unit], rmr.at[k, unit], zdown).wait_send()
        return 0

    lax.fori_loop(0, UNITS, finish, 0)


def shards(hidden, out_grad, weight, adapter_down_factor, adapter_up_factor):
    any_spec = pl.BlockSpec(memory_space=pl.ANY)
    vmem_spec = pl.BlockSpec(memory_space=pltpu.VMEM)
    dma = pltpu.SemaphoreType.DMA
    hg, rec, gd, gu = pl.pallas_call(
        kernel,
        out_shape=(
            jax.ShapeDtypeStruct((16, FF), BF),
            jax.ShapeDtypeStruct((16, 2048), BF),
            jax.ShapeDtypeStruct((16, WIN), F32),
            jax.ShapeDtypeStruct((16, 256), F32),
        ),
        in_specs=[any_spec] * 5,
        out_specs=(vmem_spec,) * 4,
        scratch_shapes=[
            pltpu.VMEM((FF, FEAT), BF),
            pltpu.VMEM((TOK, FF), BF),
            pltpu.VMEM((TOK, FEAT), BF),
            pltpu.VMEM((TOK, FF), BF),
            pltpu.VMEM((TOK, FEAT), F32),
            pltpu.VMEM((TOK, FEAT), BF),
            pltpu.VMEM((8, 16, FF), BF),
            pltpu.VMEM((7, 16, FF), BF),
            pltpu.VMEM((FF, 16), BF),
            pltpu.VMEM((16, FF), BF),
            pltpu.VMEM((16, FEAT), BF),
            pltpu.VMEM((16, 16, TOK), F32),
            pltpu.VMEM((8, 16, TOK), F32),
            pltpu.VMEM((16, TOK), BF),
            pltpu.VMEM((16, TOK), BF),
            pltpu.VMEM((4, 16, WIN), F32),
            pltpu.VMEM((3, 16, WIN), F32),
            pltpu.VMEM((4, 16, 256), F32),
            pltpu.VMEM((3, 16, 256), F32),
            pltpu.VMEM((8, 2, 16, FEAT), BF),
            pltpu.VMEM((16, FEAT), BF),
            pltpu.VMEM((16, FEAT), BF),
            dma((11,)),
            dma((2, UNITS)), dma((2, UNITS)),
            dma((2, UNITS)), dma((2, UNITS)),
            dma((2, 8)), dma((2, 8)),
            dma, dma,
            dma((2,)), dma((2,)),
            dma((2, 8)), dma((2, 8)),
            dma((7,)), dma((7,)),
            dma((2, 3)), dma((2, 3)),
            dma((8, UNITS)), dma((8, UNITS)),
            dma((7, UNITS)), dma((7, UNITS)),
            dma, dma,
            dma, dma,
        ],
        compiler_params=pltpu.CompilerParams(
            collective_id=0, has_side_effects=True, vmem_limit_bytes=48 * 1024 * 1024
        ),
    )(hidden, out_grad, weight, adapter_down_factor, adapter_up_factor)
    offset = lax.rem(lax.axis_index("gz"), 4) * 32
    grad_down = lax.dynamic_slice_in_dim(gd, offset, FF // 8, 1).T
    return hg, rec, grad_down, gu


def solution(mesh):
    placed = (
        P(("gz", "gy"), "gx"),
        P(("gz", "gx"), "gy"),
        P("gx", ("gy", "gz")),
        P("gx", None),
        P(None, "gy"),
    )
    return jax.shard_map(
        shards,
        mesh=mesh,
        in_specs=placed,
        out_specs=(
            P(("gz", "gy"), "gx"),
            P(("gz", "gx"), "gy"),
            P(("gx", "gz"), None),
            P(None, ("gy", "gz")),
        ),
        check_vma=False,
    )
```

```python
import functools

import jax
import jax.numpy as jnp
from jax import lax
from jax.experimental import pallas as pl
from jax.experimental.pallas import tpu as pltpu
from jax.sharding import PartitionSpec as P

MESH = pl.DeviceIdType.MESH
BF = jnp.bfloat16
F32 = jnp.float32

FF = 3328
UNIT = 256
UNITS = FF // UNIT
HALF = UNIT // 2
TOK = 256
FEAT = 1024
AHEAD = 4
CLASS_LAG = 5
END_LAG = 8
WIN = 512


def nt(left, right):
    return lax.dot_general(left, right, (((1,), (1,)), ((), ())), preferred_element_type=F32)


def nn(left, right):
    return jnp.dot(left, right, preferred_element_type=F32)


def mod(value, size):
    return lax.rem(value + size, size)


def rows16(block):
    return pl.ds(pl.multiple_of(block * 16, 16), 16)


def unit_cols(unit):
    return pl.ds(pl.multiple_of(unit * UNIT, UNIT), UNIT)


def kernel(
    hid, og, w, adt, au,
    hg, rec, gd, gu,
    W, H, G, I, O, Ob, R1, R2, ADT, AU, PD, PU, DT, UT, GDs, GDr, GUs, GUr, OXn, OXf, OPs, OPr,
    lsem, wds, wdr, wfs, wfr, hs, hr, gzs, gzr, gxs, gxr, pds, pdr, pus, pur, gys, gyr,
    r1s, r1r, r2s, r2r, oxs, oxr, ops_, opr,
):
    gx, gy, gz = lax.axis_index("gx"), lax.axis_index("gy"), lax.axis_index("gz")
    y, zh = lax.div(gz, 2), lax.rem(gz, 2)
    z = zh * 8 + gy
    zc, zm = lax.rem(z, 4), lax.div(z, 4)

    def zdev(step):
        where = mod(z + step, 16)
        return {"gy": lax.rem(where, 8), "gz": y * 2 + lax.div(where, 8)}

    def ydev(where):
        return {"gz": where * 2 + zh}

    def xdev(step):
        return {"gx": mod(gx + step, 8)}

    yup, ydown, yfar = mod(y + 1, 4), mod(y - 1, 4), mod(y + 2, 4)
    partner = {"gz": y * 2 + (1 - zh)}

    def remote(src, dst, ssem, rsem, to):
        return pltpu.make_async_remote_copy(
            src_ref=src, dst_ref=dst, send_sem=ssem, recv_sem=rsem, device_id=to, device_id_type=MESH
        )

    def got(part, sem):
        remote(part, part, sem, sem, xdev(1)).wait_recv()

    def left(part, sem):
        remote(part, part, sem, sem, xdev(1)).wait_send()

    def rows_of(where):
        return rows16(lax.rem(where, 4) * 4 + lax.div(where, 4))

    def quarter(q, which):
        return pl.ds(pl.multiple_of((2 * q + which) * 256, 256), 256)

    def cols_of(where):
        return pl.ds(pl.multiple_of(where * 256, 256), 256)

    my_cols = cols_of(y)
    mine = rows_of(zh * 8 + gx)
    theirs = rows_of((1 - zh) * 8 + gx)

    loads = [
        pltpu.make_async_copy(hid, H.at[rows_of(z), :], lsem.at[0]),
        pltpu.make_async_copy(w, W.at[:, my_cols], lsem.at[1]),
        pltpu.make_async_copy(adt, ADT, lsem.at[2]),
    ]
    for q in range(4):
        loads.append(pltpu.make_async_copy(og.at[:, quarter(q, zh)], G.at[mine, q * 256:(q + 1) * 256], lsem.at[3 + q]))
        loads.append(pltpu.make_async_copy(au.at[:, quarter(q, zh)], AU.at[:, q * 256:(q + 1) * 256], lsem.at[7 + q]))
    for load in loads:
        load.start()

    barrier = pltpu.get_barrier_semaphore()
    peers = [zdev(i) for i in (1, -1, 2, -2, 4, -4, 8)] + [ydev(yup), ydev(ydown), ydev(yfar)]
    peers += [xdev(i) for i in range(1, 8)]
    for peer in peers:
        pl.semaphore_signal(barrier, inc=1, device_id=peer, device_id_type=MESH)
    pl.semaphore_wait(barrier, len(peers))

    def w_rows(unit):
        return pl.ds(pl.multiple_of(unit * UNIT, UNIT), UNIT)

    def w_half(unit, side):
        return pl.ds(pl.multiple_of(unit * UNIT + side * HALF, HALF), HALF)

    def w_direct(unit, side):
        return remote(
            w.at[w_rows(unit), :], W.at[w_rows(unit), my_cols], wds.at[side], wdr.at[side, unit],
            ydev(yup if side == 0 else ydown),
        )

    def w_pass(unit, side):
        part = W.at[w_half(unit, side), cols_of(ydown if side == 0 else yup)]
        return remote(part, part, wfs.at[side], wfr.at[side, unit], ydev(yup if side == 0 else ydown))

    def w_step(unit):
        @pl.when(unit + AHEAD < UNITS)
        def _():
            w_direct(unit + AHEAD, 0).start()
            w_direct(unit + AHEAD, 1).start()

        for side in range(2):
            got(W.at[w_rows(unit), cols_of(ydown if side == 0 else yup)], wdr.at[side, unit])
            w_pass(unit, side).start()

    for unit in range(AHEAD):
        w_direct(unit, 0).start()
        w_direct(unit, 1).start()

    for q in range(4):
        remote(og.at[:, quarter(q, 1 - zh)], G.at[mine, q * 256:(q + 1) * 256], gzs, gzr, partner).start()

    def h_move(step, side):
        part = H.at[rows_of(mod(z - step if side == 0 else z + step, 16)), :]
        return remote(part, part, hs.at[side], hr.at[side, step], zdev(1 if side == 0 else -1))

    def h_step(step):
        got(H.at[rows_of(mod(z - 1 - step, 16)), :], hr.at[0, step])

        @pl.when(step < 7)
        def _():
            h_move(step + 1, 0).start()
            got(H.at[rows_of(mod(z + 1 + step, 16)), :], hr.at[1, step])

        @pl.when(step < 6)
        def _():
            h_move(step + 1, 1).start()

    loads[0].wait()
    h_move(0, 0).start()
    h_move(0, 1).start()

    def g_send(i, rows, which):
        return remote(G.at[rows, :], G.at[rows, :], gxs.at[which], gxr.at[which], xdev(i))

    for load in loads[2:]:
        load.wait()
    for i in range(1, 8):
        g_send(i, mine, 0).start()
    O[...] = jnp.zeros_like(O)
    loads[1].wait()

    pd_steps = ((1, -1, 2), (4, -4, 8))

    def pd_send(stage, i):
        return remote(
            PD.at[stage, 0], PD.at[stage, i + 1], pds.at[stage, i], pdr.at[stage, i], zdev(pd_steps[stage][i])
        )

    def pd_sum(stage):
        for i in range(3):
            got(PD.at[stage, i + 1], pdr.at[stage, i])
        return PD[stage, 0] + PD[stage, 1] + PD[stage, 2] + PD[stage, 3]

    def pu_send(i):
        return remote(PU.at[0], PU.at[i], pus, pur.at[i - 1], xdev(i))

    def up_unit(unit, total):
        return total + nt(ADT[:, unit_cols(unit)], H[:, unit_cols(unit)])

    def window(where):
        block = 2 * where + zh
        return pl.ds(pl.multiple_of(lax.div(block * 13, 4) * 128, 128), WIN)

    def gy_send(kind, i):
        src, dst = (GDs.at[i - 1], GDr.at[i - 1]) if kind == 0 else (GUs.at[i - 1], GUr.at[i - 1])
        return remote(src, dst, gys.at[kind, i - 1], gyr.at[kind, i - 1], ydev(mod(y + i, 4)))

    class_rows = pl.ds(pl.multiple_of(zc * 64, 64), 64)

    def r1_send(unit, i):
        step = (1, -1, 2 - 4 * lax.rem(unit, 2))[i]
        rows = pl.ds(pl.multiple_of(lax.rem(z + step + 16, 4) * 64, 64), 64)
        cols = unit_cols(unit)
        return remote(I.at[rows, cols], R1.at[i, :, cols], r1s.at[i], r1r.at[i, unit], zdev(step))

    def r2_send(unit, i):
        rows = rows16(lax.rem(zm + i + 1, 4))
        cols = unit_cols(unit)
        return remote(
            R1.at[0, rows, cols], R2.at[i, :, cols], r2s.at[i], r2r.at[i, unit], zdev((4, 8, -4)[i])
        )

    def input_unit(unit):
        for side in range(2):
            got(W.at[w_half(unit, side), cols_of(yfar)], wfr.at[side, unit])
        I[:, unit_cols(unit)] = nt(G[...], W[w_rows(unit), :]).astype(BF)
        for i in range(3):
            r1_send(unit, i).start()

    def input_class(unit):
        cols = unit_cols(unit)
        for i in range(3):
            got(R1.at[i, :, cols], r1r.at[i, unit])
        total = I[class_rows, cols].astype(F32)
        for i in range(3):
            total = total + R1[i, :, cols].astype(F32)
        R1[0, :, cols] = total.astype(BF)
        for i in range(3):
            r2_send(unit, i).start()

    def pick(where):
        first = (lax.rem(where, 4) * 4 + lax.div(where, 4)) * 16
        return (
            lax.broadcasted_iota(jnp.int32, (16, TOK), 1) == lax.broadcasted_iota(jnp.int32, (16, TOK), 0) + first
        ).astype(BF)

    def input_end(unit):
        cols = unit_cols(unit)
        for i in range(3):
            got(R2.at[i, :, cols], r2r.at[i, unit])
        total = R1[0, rows16(zm), cols].astype(F32)
        for i in range(3):
            total = total + R2[i, :, cols].astype(F32)
        low = nt(pick(z), DT[...]).astype(BF)
        hg[:, cols] = (total + 2.0 * nn(low, ADT[:, cols])).astype(BF)

    order = (0, 1, 3, 2)

    def output_unit(places, unit):
        block = H[:, unit_cols(unit)]
        for q in places:
            O[:, q * 256:(q + 1) * 256] += nn(block, W[w_rows(unit), cols_of(mod(y + order[q], 4))])

    def ox_send(far, i, which):
        to = mod(gx + i, 8)
        rows = rows_of(which * 8 + to)
        src = Ob.at[rows, 768:1024] if far else Ob.at[rows, 0:768]
        return remote(src, (OXf if far else OXn).at[i, which], oxs.at[far], oxr.at[far], xdev(i))

    def ox_go(far):
        lo, hi = (768, 1024) if far else (0, 768)
        Ob[:, lo:hi] = O[:, lo:hi].astype(BF)
        for i in range(1, 8):
            for which in range(2):
                ox_send(far, i, which).start()

    def op_send(far):
        lo, hi = (768, 1024) if far else (0, 768)
        return remote(OPs.at[:, lo:hi], OPr.at[:, lo:hi], ops_.at[far], opr.at[far], partner)

    def ox_sum(far):
        lo, hi = (768, 1024) if far else (0, 768)
        OX = OXf if far else OXn
        got(OX.at[1:8], oxr.at[far])
        for which, half in ((0, 1 - zh), (1, zh)):
            total = O[rows_of(half * 8 + gx), lo:hi]
            for i in range(1, 8):
                total = total + OX[i, half].astype(F32)
            low = nt(pick(half * 8 + gx), UT[...]).astype(BF)
            for q in range(lo // 256, hi // 256):
                factor = AU[:, cols_of(mod(y + order[q], 4))]
                part = total[:, q * 256 - lo:(q + 1) * 256 - lo]
                part = (part + 2.0 * nn(low, factor)).astype(BF)
                if which == 0:
                    OPs[:, q * 256:(q + 1) * 256] = part
                else:
                    rec[:, quarter(mod(y + order[q], 4), zh)] = part
            if which == 0:
                op_send(far).start()

    def op_end(far):
        lo, hi = (768, 1024) if far else (0, 768)
        got(OPr.at[:, lo:hi], opr.at[far])
        for q in range(lo // 256, hi // 256):
            rec[:, quarter(mod(y + order[q], 4), 1 - zh)] = OPr[:, q * 256:(q + 1) * 256]

    def loop(j, _):
        @pl.when(j < 8)
        def _():
            h_step(j)

        @pl.when(j == 1)
        def _():
            got(G.at[theirs, :], gzr)
            for i in range(1, 8):
                g_send(i, theirs, 1).start()

        w_step(j)

        @pl.when(j == 2)
        def _():
            for which in range(2):
                got(G.at[0:112, :], gxr.at[which])
            PD[0, 0] = nt(AU[...], G[...])
            for i in range(3):
                pd_send(0, i).start()

        first = lax.min(3 * (j - 8), UNITS - 1)
        last = lax.min(3 * (j - 7), UNITS)

        @pl.when(j >= 8)
        def _():
            def near(unit, _):
                output_unit((0, 1, 2), unit)
                return 0

            lax.fori_loop(first, last, near, 0)

        @pl.when(j == UNITS - 1)
        def _():
            ox_go(0)

        @pl.when(j >= 2)
        def _():
            input_unit(j - 2)

        far_first = lax.min(4 * (j - 9), j - 2)
        far_last = lax.min(4 * (j - 8), j - 1)

        @pl.when(j >= 9)
        def _():
            def far(unit, _):
                output_unit((3,), unit)
                return 0

            lax.fori_loop(far_first, far_last, far, 0)

        @pl.when(j == 3)
        def _():
            PD[1, 0] = pd_sum(0)
            for i in range(3):
                pd_send(1, i).start()

        @pl.when(j == 4)
        def _():
            DT[...] = pd_sum(1).astype(BF)

        @pl.when(j >= CLASS_LAG)
        def _():
            input_class(j - CLASS_LAG)

        @pl.when(j >= END_LAG)
        def _():
            input_end(j - END_LAG)

        @pl.when(j == 8)
        def _():
            PU[0] = lax.fori_loop(0, UNITS, up_unit, jnp.zeros((16, TOK), F32))
            for i in range(1, 8):
                pu_send(i).start()
            for i in range(1, 4):
                GDs[i - 1] = nn(DT[...], H[:, window(mod(y + i, 4))]).astype(BF)
                gy_send(0, i).start()

        @pl.when(j == 9)
        def _():
            total = PU[0]
            for i in range(1, 8):
                got(PU.at[i], pur.at[i - 1])
                total = total + PU[i]
            UT[...] = total.astype(BF)
            for i in range(1, 4):
                GUs[i - 1] = nn(UT[...], G[:, cols_of(mod(y + i, 4))]).astype(BF)
                gy_send(1, i).start()

        @pl.when(j == 11)
        def _():
            total_down = nn(DT[...], H[:, window(y)])
            total_up = nn(UT[...], G[:, my_cols])
            for i in range(1, 4):
                got(GDr.at[i - 1], gyr.at[0, i - 1])
                got(GUr.at[i - 1], gyr.at[1, i - 1])
                total_down = total_down + GDr[i - 1].astype(F32)
                total_up = total_up + GUr[i - 1].astype(F32)
            gd[...] = total_down * (2.0 / 1024)
            gu[...] = total_up * (2.0 / 1024)

        return 0

    lax.fori_loop(0, UNITS, loop, 0)

    def over(first, last, work):
        def body(unit, _):
            work(unit)
            return 0

        lax.fori_loop(first, last, body, 0)

    def last_unit(unit):
        input_unit(unit)
        output_unit((3,), unit)

    over(UNITS - 2, UNITS, last_unit)
    ox_go(1)
    over(UNITS - CLASS_LAG, UNITS - 1, input_class)
    ox_sum(0)
    over(UNITS - 1, UNITS, input_class)
    over(UNITS - END_LAG, UNITS - 1, input_end)
    ox_sum(1)
    over(UNITS - 1, UNITS, input_end)

    left(G.at[mine, :], gzs)
    for which in range(2):
        left(G.at[0:112, :], gxs.at[which])
    left(PU.at[1:8], pus)
    for i in range(3):
        for stage in range(2):
            pd_send(stage, i).wait_send()
            gy_send(stage, i + 1).wait_send()
        left(I.at[0:64, :], r1s.at[i])
        left(I.at[0:16, :], r2s.at[i])
    left(H.at[0:128, :], hs.at[0])
    left(H.at[0:112, :], hs.at[1])
    for side in range(2):
        left(W.at[:, 0:256], wds.at[side])
        left(W.at[0:FF // 2, 0:256], wfs.at[side])
    left(OXn.at[1:8], oxs.at[0])
    left(OXf.at[1:8], oxs.at[1])
    for far in range(2):
        op_end(far)
        op_send(far).wait_send()


def shards(hidden, out_grad, weight, adapter_down_factor, adapter_up_factor):
    any_spec = pl.BlockSpec(memory_space=pl.ANY)
    vmem_spec = pl.BlockSpec(memory_space=pltpu.VMEM)
    dma = pltpu.SemaphoreType.DMA
    hg, rec, gd, gu = pl.pallas_call(
        kernel,
        out_shape=(
            jax.ShapeDtypeStruct((16, FF), BF),
            jax.ShapeDtypeStruct((16, 2048), BF),
            jax.ShapeDtypeStruct((16, WIN), F32),
            jax.ShapeDtypeStruct((16, 256), F32),
        ),
        in_specs=[any_spec] * 5,
        out_specs=(vmem_spec,) * 4,
        scratch_shapes=[
            pltpu.VMEM((FF, FEAT), BF),
            pltpu.VMEM((TOK, FF), BF),
            pltpu.VMEM((TOK, FEAT), BF),
            pltpu.VMEM((TOK, FF), BF),
            pltpu.VMEM((TOK, FEAT), F32),
            pltpu.VMEM((TOK, FEAT), BF),
            pltpu.VMEM((3, 64, FF), BF),
            pltpu.VMEM((3, 16, FF), BF),
            pltpu.VMEM((16, FF), BF),
            pltpu.VMEM((16, FEAT), BF),
            pltpu.VMEM((2, 4, 16, TOK), F32),
            pltpu.VMEM((8, 16, TOK), F32),
            pltpu.VMEM((16, TOK), BF),
            pltpu.VMEM((16, TOK), BF),
            pltpu.VMEM((3, 16, WIN), BF),
            pltpu.VMEM((3, 16, WIN), BF),
            pltpu.VMEM((3, 16, 256), BF),
            pltpu.VMEM((3, 16, 256), BF),
            pltpu.VMEM((8, 2, 16, 768), BF),
            pltpu.VMEM((8, 2, 16, 256), BF),
            pltpu.VMEM((16, FEAT), BF),
            pltpu.VMEM((16, FEAT), BF),
            dma((11,)),
            dma((2,)), dma((2, UNITS)),
            dma((2,)), dma((2, UNITS)),
            dma((2,)), dma((2, 8)),
            dma, dma,
            dma((2,)), dma((2,)),
            dma((2, 3)), dma((2, 3)),
            dma, dma((7,)),
            dma((2, 3)), dma((2, 3)),
            dma((3,)), dma((3, UNITS)),
            dma((3,)), dma((3, UNITS)),
            dma((2,)), dma((2,)),
            dma((2,)), dma((2,)),
        ],
        compiler_params=pltpu.CompilerParams(
            collective_id=0, has_side_effects=True, vmem_limit_bytes=63 * 1024 * 1024
        ),
    )(hidden, out_grad, weight, adapter_down_factor.T, adapter_up_factor)
    offset = lax.rem(lax.axis_index("gz"), 4) * 32
    grad_down = lax.dynamic_slice_in_dim(gd, offset, FF // 8, 1).T
    return hg, rec, grad_down, gu


def solution(mesh):
    placed = (
        P(("gz", "gy"), "gx"),
        P(("gz", "gx"), "gy"),
        P("gx", ("gy", "gz")),
        P("gx", None),
        P(None, "gy"),
    )
    return jax.shard_map(
        shards,
        mesh=mesh,
        in_specs=placed,
        out_specs=(
            P(("gz", "gy"), "gx"),
            P(("gz", "gx"), "gy"),
            P(("gx", "gz"), None),
            P(None, ("gy", "gz")),
        ),
        check_vma=False,
    )
```

```python
import functools

import jax
import jax.numpy as jnp
from jax import lax
from jax.experimental import pallas as pl
from jax.experimental.pallas import tpu as pltpu
from jax.sharding import PartitionSpec as P

MESH = pl.DeviceIdType.MESH
BF = jnp.bfloat16
F32 = jnp.float32

FF = 3328
UNIT = 256
UNITS = FF // UNIT
CHUNK = 128
CHUNKS = FF // CHUNK
HALF = CHUNK // 2
TOK = 256
FEAT = 1024
AHEAD = 5
CLASS_LEFT = 3
END_LAG = 8
H_LAG = 1
WIN = 512


def nt(left, right):
    return lax.dot_general(left, right, (((1,), (1,)), ((), ())), preferred_element_type=F32)


def nn(left, right):
    return jnp.dot(left, right, preferred_element_type=F32)


def mod(value, size):
    return lax.rem(value + size, size)


def rows16(block):
    return pl.ds(pl.multiple_of(block * 16, 16), 16)


def unit_cols(unit):
    return pl.ds(pl.multiple_of(unit * UNIT, UNIT), UNIT)


def kernel(
    hid, og, w, adt, au,
    hg, rec, gd, gu,
    W, H, G, I, O, Ob, R1, R2, ADT, AU, PD, PU, DT, UT, GDs, GDr, GUs, GUr, OXn, OXf, OPs, OPr, LOW, LOWO,
    lsem, wds, wdr, wfs, wfr, hs, hr, gzs, gzr, gxs, gxr, pds, pdr, pus, pur, gys, gyr,
    r1s, r1r, r2s, r2r, oxs, oxr, ops_, opr,
):
    gx, gy, gz = lax.axis_index("gx"), lax.axis_index("gy"), lax.axis_index("gz")
    y, zh = lax.div(gz, 2), lax.rem(gz, 2)
    z = zh * 8 + gy
    zc, zm = lax.rem(z, 4), lax.div(z, 4)

    def zdev(step):
        where = mod(z + step, 16)
        return {"gy": lax.rem(where, 8), "gz": y * 2 + lax.div(where, 8)}

    def ydev(where):
        return {"gz": where * 2 + zh}

    def xdev(step):
        return {"gx": mod(gx + step, 8)}

    yup, ydown, yfar = mod(y + 1, 4), mod(y - 1, 4), mod(y + 2, 4)
    partner = {"gz": y * 2 + (1 - zh)}

    def remote(src, dst, ssem, rsem, to):
        return pltpu.make_async_remote_copy(
            src_ref=src, dst_ref=dst, send_sem=ssem, recv_sem=rsem, device_id=to, device_id_type=MESH
        )

    def got(part, sem):
        remote(part, part, sem, sem, xdev(1)).wait_recv()

    def left(part, sem):
        remote(part, part, sem, sem, xdev(1)).wait_send()

    def rows_of(where):
        return rows16(lax.rem(where, 4) * 4 + lax.div(where, 4))

    def quarter(q, which):
        return pl.ds(pl.multiple_of((2 * q + which) * 256, 256), 256)

    def cols_of(where):
        return pl.ds(pl.multiple_of(where * 256, 256), 256)

    my_cols = cols_of(y)
    mine = rows_of(zh * 8 + gx)
    theirs = rows_of((1 - zh) * 8 + gx)

    loads = [
        pltpu.make_async_copy(hid, H.at[rows_of(z), :], lsem.at[0]),
        pltpu.make_async_copy(w, W.at[:, my_cols], lsem.at[1]),
        pltpu.make_async_copy(adt, ADT, lsem.at[2]),
    ]
    for q in range(4):
        loads.append(pltpu.make_async_copy(og.at[:, quarter(q, zh)], G.at[mine, q * 256:(q + 1) * 256], lsem.at[3 + q]))
        loads.append(pltpu.make_async_copy(au.at[:, quarter(q, zh)], AU.at[:, q * 256:(q + 1) * 256], lsem.at[7 + q]))
    for load in loads:
        load.start()

    barrier = pltpu.get_barrier_semaphore()
    peers = [zdev(i) for i in (1, -1, 2, -2, 4, -4, 8)] + [ydev(yup), ydev(ydown), ydev(yfar)]
    peers += [xdev(i) for i in range(1, 8)]
    for peer in peers:
        pl.semaphore_signal(barrier, inc=1, device_id=peer, device_id_type=MESH)
    pl.semaphore_wait(barrier, len(peers))

    def w_rows(unit):
        return pl.ds(pl.multiple_of(unit * UNIT, UNIT), UNIT)

    def w_chunk(chunk):
        return pl.ds(pl.multiple_of(chunk * CHUNK, CHUNK), CHUNK)

    def w_half(chunk, side):
        return pl.ds(pl.multiple_of(chunk * CHUNK + side * HALF, HALF), HALF)

    def w_direct(unit, side):
        return remote(
            w.at[w_chunk(unit), :], W.at[w_chunk(unit), my_cols], wds.at[side], wdr.at[side, unit],
            ydev(yup if side == 0 else ydown),
        )

    def w_pass(unit, side):
        part = W.at[w_half(unit, side), cols_of(ydown if side == 0 else yup)]
        return remote(part, part, wfs.at[side], wfr.at[side, unit], ydev(yup if side == 0 else ydown))

    def w_step(unit):
        @pl.when(unit + AHEAD < CHUNKS)
        def _():
            w_direct(unit + AHEAD, 0).start()
            w_direct(unit + AHEAD, 1).start()

        for side in range(2):
            got(W.at[w_chunk(unit), cols_of(ydown if side == 0 else yup)], wdr.at[side, unit])
            w_pass(unit, side).start()

    for unit in range(AHEAD):
        w_direct(unit, 0).start()
        w_direct(unit, 1).start()

    for q in range(4):
        remote(og.at[:, quarter(q, 1 - zh)], G.at[mine, q * 256:(q + 1) * 256], gzs, gzr, partner).start()

    def h_move(step, side):
        part = H.at[rows_of(mod(z - step if side == 0 else z + step, 16)), :]
        return remote(part, part, hs.at[side], hr.at[side, step], zdev(1 if side == 0 else -1))

    def h_step(step):
        got(H.at[rows_of(mod(z - 1 - step, 16)), :], hr.at[0, step])

        @pl.when(step < 7)
        def _():
            h_move(step + 1, 0).start()
            got(H.at[rows_of(mod(z + 1 + step, 16)), :], hr.at[1, step])

        @pl.when(step < 6)
        def _():
            h_move(step + 1, 1).start()

    loads[0].wait()
    h_move(0, 0).start()
    h_move(0, 1).start()

    def g_send(i, rows, which):
        return remote(G.at[rows, :], G.at[rows, :], gxs.at[which], gxr.at[which], xdev(i))

    for load in loads[2:]:
        load.wait()
    for i in range(1, 8):
        g_send(i, mine, 0).start()
    O[...] = jnp.zeros_like(O)
    loads[1].wait()

    pd_steps = ((1, -1, 2), (4, -4, 8))

    def pd_send(stage, i):
        return remote(
            PD.at[stage, 0], PD.at[stage, i + 1], pds.at[stage, i], pdr.at[stage, i], zdev(pd_steps[stage][i])
        )

    def pd_sum(stage):
        for i in range(3):
            got(PD.at[stage, i + 1], pdr.at[stage, i])
        return sum(PD[stage, i].astype(F32) for i in range(4))

    def pu_send(i):
        return remote(PU.at[0], PU.at[i], pus, pur.at[i - 1], xdev(i))

    def up_unit(unit, total):
        return total + nt(ADT[:, unit_cols(unit)], H[:, unit_cols(unit)])

    def window(where):
        block = 2 * where + zh
        return pl.ds(pl.multiple_of(lax.div(block * 13, 4) * 128, 128), WIN)

    def gy_send(kind, i):
        src, dst = (GDs.at[i - 1], GDr.at[i - 1]) if kind == 0 else (GUs.at[i - 1], GUr.at[i - 1])
        return remote(src, dst, gys.at[kind, i - 1], gyr.at[kind, i - 1], ydev(mod(y + i, 4)))

    class_rows = pl.ds(pl.multiple_of(zc * 64, 64), 64)

    def r1_send(unit, i):
        step = (1, -1, 2 - 4 * lax.rem(unit, 2))[i]
        rows = pl.ds(pl.multiple_of(lax.rem(z + step + 16, 4) * 64, 64), 64)
        cols = unit_cols(unit)
        return remote(I.at[rows, cols], R1.at[i, :, cols], r1s.at[i], r1r.at[i, unit], zdev(step))

    def r2_send(unit, i):
        rows = rows16(lax.rem(zm + i + 1, 4))
        cols = unit_cols(unit)
        return remote(
            R1.at[0, rows, cols], R2.at[i, :, cols], r2s.at[i], r2r.at[i, unit], zdev((4, 8, -4)[i])
        )

    def input_unit(unit):
        for side in range(2):
            for chunk in (2 * unit, 2 * unit + 1):
                got(W.at[w_half(chunk, side), cols_of(yfar)], wfr.at[side, chunk])
        I[:, unit_cols(unit)] = nt(G[...], W[w_rows(unit), :]).astype(BF)
        for i in range(3):
            r1_send(unit, i).start()

    def input_class(unit):
        cols = unit_cols(unit)
        for i in range(3):
            got(R1.at[i, :, cols], r1r.at[i, unit])
        total = I[class_rows, cols].astype(F32)
        for i in range(3):
            total = total + R1[i, :, cols].astype(F32)
        R1[0, :, cols] = total.astype(BF)
        for i in range(3):
            r2_send(unit, i).start()

    def pick(where):
        first = (lax.rem(where, 4) * 4 + lax.div(where, 4)) * 16
        return (
            lax.broadcasted_iota(jnp.int32, (16, TOK), 1) == lax.broadcasted_iota(jnp.int32, (16, TOK), 0) + first
        ).astype(BF)

    def input_end(unit):
        cols = unit_cols(unit)
        for i in range(3):
            got(R2.at[i, :, cols], r2r.at[i, unit])
        total = R1[0, rows16(zm), cols].astype(F32)
        for i in range(3):
            total = total + R2[i, :, cols].astype(F32)
        hg[:, cols] = (total + LOW[:, cols]).astype(BF)

    order = (0, 1, 3, 2)

    def output_unit(places, unit):
        block = H[:, unit_cols(unit)]
        for q in places:
            O[:, q * 256:(q + 1) * 256] += nn(block, W[w_rows(unit), cols_of(mod(y + order[q], 4))])

    def ox_send(far, i, which):
        to = mod(gx + i, 8)
        rows = rows_of(which * 8 + to)
        src = Ob.at[rows, 768:1024] if far else Ob.at[rows, 0:768]
        return remote(src, (OXf if far else OXn).at[i, which], oxs.at[far], oxr.at[far], xdev(i))

    def ox_go(far):
        lo, hi = (768, 1024) if far else (0, 768)
        Ob[:, lo:hi] = O[:, lo:hi].astype(BF)
        for i in range(1, 8):
            for which in range(2):
                ox_send(far, i, which).start()

    def op_send(far):
        lo, hi = (768, 1024) if far else (0, 768)
        return remote(OPs.at[:, lo:hi], OPr.at[:, lo:hi], ops_.at[far], opr.at[far], partner)

    def ox_sum(far):
        lo, hi = (768, 1024) if far else (0, 768)
        OX = OXf if far else OXn
        got(OX.at[1:8], oxr.at[far])
        for which, half in ((0, 1 - zh), (1, zh)):
            total = O[rows_of(half * 8 + gx), lo:hi]
            for i in range(1, 8):
                total = total + OX[i, half].astype(F32)
            total = (total + LOWO[which, :, lo:hi]).astype(BF)
            for q in range(lo // 256, hi // 256):
                part = total[:, q * 256 - lo:(q + 1) * 256 - lo]
                if which == 0:
                    OPs[:, q * 256:(q + 1) * 256] = part
                else:
                    rec[:, quarter(mod(y + order[q], 4), zh)] = part
            if which == 0:
                op_send(far).start()

    def op_end(far):
        lo, hi = (768, 1024) if far else (0, 768)
        got(OPr.at[:, lo:hi], opr.at[far])
        for q in range(lo // 256, hi // 256):
            rec[:, quarter(mod(y + order[q], 4), 1 - zh)] = OPr[:, q * 256:(q + 1) * 256]

    def loop(j, _):
        w_step(2 * j)

        @pl.when((j >= H_LAG) & (j < 8 + H_LAG))
        def _():
            h_step(j - H_LAG)

        @pl.when(j == 1)
        def _():
            got(G.at[theirs, :], gzr)
            for i in range(1, 8):
                g_send(i, theirs, 1).start()

        w_step(2 * j + 1)

        @pl.when(j == 2)
        def _():
            for which in range(2):
                got(G.at[0:112, :], gxr.at[which])
            PD[0, 0] = nt(AU[...], G[...]).astype(BF)
            for i in range(3):
                pd_send(0, i).start()

        first = lax.min(4 * (j - 9), UNITS - 1)
        last = lax.min(4 * (j - 8), UNITS)

        @pl.when(j >= 9)
        def _():
            def near(unit, _):
                output_unit((0, 1, 2), unit)
                return 0

            lax.fori_loop(first, last, near, 0)

        @pl.when(j == UNITS - 1)
        def _():
            ox_go(0)

        @pl.when(j >= 2)
        def _():
            input_unit(j - 2)

        far_first = lax.min(4 * (j - 9), j - 2)
        far_last = lax.min(4 * (j - 8), j - 1)

        @pl.when(j >= 9)
        def _():
            def far(unit, _):
                output_unit((3,), unit)
                return 0

            lax.fori_loop(far_first, far_last, far, 0)

        @pl.when(j == 3)
        def _():
            PD[1, 0] = pd_sum(0).astype(BF)
            for i in range(3):
                pd_send(1, i).start()

        @pl.when(j == 4)
        def _():
            DT[...] = pd_sum(1).astype(BF)

        def classes(turn):
            late = (turn >= 10).astype(jnp.int32) + (turn >= 12).astype(jnp.int32)
            return lax.max(turn - 4 + late, 0)

        def class_body(unit, _):
            input_class(unit)
            return 0

        lax.fori_loop(classes(j - 1), classes(j), class_body, 0)

        @pl.when(j >= END_LAG)
        def _():
            input_end(j - END_LAG)

        @pl.when(j == 8 + H_LAG)
        def _():
            PU[0] = lax.fori_loop(0, UNITS, up_unit, jnp.zeros((16, TOK), F32))
            for i in range(1, 8):
                pu_send(i).start()
            for i in range(1, 4):
                GDs[i - 1] = nn(DT[...], H[:, window(mod(y + i, 4))]).astype(BF)
                gy_send(0, i).start()

        @pl.when(j == 9 + H_LAG)
        def _():
            total = PU[0]
            for i in range(1, 8):
                got(PU.at[i], pur.at[i - 1])
                total = total + PU[i]
            UT[...] = total.astype(BF)
            for i in range(1, 4):
                GUs[i - 1] = nn(UT[...], G[:, cols_of(mod(y + i, 4))]).astype(BF)
                gy_send(1, i).start()

        @pl.when(j == 5)
        def _():
            low = nt(pick(z), DT[...]).astype(BF)
            LOW[...] = 2.0 * nn(low, ADT[...])

        @pl.when(j == 10 + H_LAG)
        def _():
            for which, half in ((0, 1 - zh), (1, zh)):
                low = nt(pick(half * 8 + gx), UT[...]).astype(BF)
                for q in range(4):
                    LOWO[which, :, q * 256:(q + 1) * 256] = 2.0 * nn(low, AU[:, cols_of(mod(y + order[q], 4))])

        @pl.when(j == 11 + H_LAG)
        def _():
            total_down = nn(DT[...], H[:, window(y)])
            total_up = nn(UT[...], G[:, my_cols])
            for i in range(1, 4):
                got(GDr.at[i - 1], gyr.at[0, i - 1])
                got(GUr.at[i - 1], gyr.at[1, i - 1])
                total_down = total_down + GDr[i - 1].astype(F32)
                total_up = total_up + GUr[i - 1].astype(F32)
            gd[...] = total_down * (2.0 / 1024)
            gu[...] = total_up * (2.0 / 1024)

        return 0

    lax.fori_loop(0, UNITS, loop, 0)

    def over(first, last, work):
        def body(unit, _):
            work(unit)
            return 0

        lax.fori_loop(first, last, body, 0)

    def last_unit(unit):
        input_unit(unit)
        output_unit((3,), unit)

    over(UNITS - 2, UNITS, last_unit)
    ox_go(1)
    over(UNITS - CLASS_LEFT, UNITS - 1, input_class)
    ox_sum(0)
    over(UNITS - 1, UNITS, input_class)
    ox_sum(1)
    over(UNITS - END_LAG, UNITS - 1, input_end)

    left(G.at[mine, :], gzs)
    for which in range(2):
        left(G.at[0:112, :], gxs.at[which])
    left(PU.at[1:8], pus)
    for i in range(3):
        for stage in range(2):
            pd_send(stage, i).wait_send()
            gy_send(stage, i + 1).wait_send()
        left(I.at[0:64, :], r1s.at[i])
        left(I.at[0:16, :], r2s.at[i])
    left(H.at[0:128, :], hs.at[0])
    left(H.at[0:112, :], hs.at[1])
    for side in range(2):
        left(W.at[:, 0:256], wds.at[side])
        left(W.at[0:FF // 2, 0:256], wfs.at[side])
    left(OXn.at[1:8], oxs.at[0])
    left(OXf.at[1:8], oxs.at[1])
    over(UNITS - 1, UNITS, input_end)
    for far in range(2):
        op_end(far)
        op_send(far).wait_send()


def hand_over(hg_in, rec_in, gd_in, gu_in, hg, rec, gd, gu):
    hg[...] = hg_in[...]
    rec[...] = rec_in[...]
    gu[...] = gu_in[...]
    place = lax.rem(lax.axis_index("gz"), 4)
    for k in range(4):
        @pl.when(place == k)
        def _(k=k):
            gd[...] = gd_in[:, 32 * k:32 * k + FF // 8]


def shards(hidden, out_grad, weight, adapter_down_factor, adapter_up_factor):
    any_spec = pl.BlockSpec(memory_space=pl.ANY)
    vmem_spec = pl.BlockSpec(memory_space=pltpu.VMEM)
    dma = pltpu.SemaphoreType.DMA
    hg, rec, gd, gu = pl.pallas_call(
        kernel,
        out_shape=(
            jax.ShapeDtypeStruct((16, FF), BF),
            jax.ShapeDtypeStruct((16, 2048), BF),
            jax.ShapeDtypeStruct((16, WIN), F32),
            jax.ShapeDtypeStruct((16, 256), F32),
        ),
        in_specs=[any_spec] * 5,
        out_specs=(vmem_spec,) * 4,
        scratch_shapes=[
            pltpu.VMEM((FF, FEAT), BF),
            pltpu.VMEM((TOK, FF), BF),
            pltpu.VMEM((TOK, FEAT), BF),
            pltpu.VMEM((TOK, FF), BF),
            pltpu.VMEM((TOK, FEAT), F32),
            pltpu.VMEM((TOK, FEAT), BF),
            pltpu.VMEM((3, 64, FF), BF),
            pltpu.VMEM((3, 16, FF), BF),
            pltpu.VMEM((16, FF), BF),
            pltpu.VMEM((16, FEAT), BF),
            pltpu.VMEM((2, 4, 16, TOK), BF),
            pltpu.VMEM((8, 16, TOK), F32),
            pltpu.VMEM((16, TOK), BF),
            pltpu.VMEM((16, TOK), BF),
            pltpu.VMEM((3, 16, WIN), BF),
            pltpu.VMEM((3, 16, WIN), BF),
            pltpu.VMEM((3, 16, 256), BF),
            pltpu.VMEM((3, 16, 256), BF),
            pltpu.VMEM((8, 2, 16, 768), BF),
            pltpu.VMEM((8, 2, 16, 256), BF),
            pltpu.VMEM((16, FEAT), BF),
            pltpu.VMEM((16, FEAT), BF),
            pltpu.VMEM((16, FF), F32),
            pltpu.VMEM((2, 16, FEAT), F32),
            dma((11,)),
            dma((2,)), dma((2, CHUNKS)),
            dma((2,)), dma((2, CHUNKS)),
            dma((2,)), dma((2, 8)),
            dma, dma,
            dma((2,)), dma((2,)),
            dma((2, 3)), dma((2, 3)),
            dma, dma((7,)),
            dma((2, 3)), dma((2, 3)),
            dma((3,)), dma((3, UNITS)),
            dma((3,)), dma((3, UNITS)),
            dma((2,)), dma((2,)),
            dma((2,)), dma((2,)),
        ],
        compiler_params=pltpu.CompilerParams(
            collective_id=0, has_side_effects=True, vmem_limit_bytes=63 * 1024 * 1024
        ),
    )(hidden, out_grad, weight, adapter_down_factor.T, adapter_up_factor)
    hg, rec, gd, gu = pl.pallas_call(
        hand_over,
        out_shape=(
            jax.ShapeDtypeStruct((16, FF), BF),
            jax.ShapeDtypeStruct((16, 2048), BF),
            jax.ShapeDtypeStruct((16, FF // 8), F32),
            jax.ShapeDtypeStruct((16, 256), F32),
        ),
        in_specs=[vmem_spec] * 4,
        out_specs=(vmem_spec,) * 4,
    )(hg, rec, gd, gu)
    return hg, rec, gd.T, gu


def solution(mesh):
    placed = (
        P(("gz", "gy"), "gx"),
        P(("gz", "gx"), "gy"),
        P("gx", ("gy", "gz")),
        P("gx", None),
        P(None, "gy"),
    )
    return jax.shard_map(
        shards,
        mesh=mesh,
        in_specs=placed,
        out_specs=(
            P(("gz", "gy"), "gx"),
            P(("gz", "gx"), "gy"),
            P(("gx", "gz"), None),
            P(None, ("gy", "gz")),
        ),
        check_vma=False,
    )
```

```python
import functools

import jax
import jax.numpy as jnp
from jax import lax
from jax.experimental import pallas as pl
from jax.experimental.pallas import tpu as pltpu
from jax.sharding import PartitionSpec as P

MESH = pl.DeviceIdType.MESH
BF = jnp.bfloat16
F32 = jnp.float32

FF = 3328
UNIT = 256
UNITS = FF // UNIT
CHUNK = 128
CHUNKS = FF // CHUNK
HALF = CHUNK // 2
TOK = 256
FEAT = 1024
AHEAD = 5
CLASS_LEFT = 3
END_LAG = 8
H_LAG = 1
WIN = 512


def nt(left, right):
    return lax.dot_general(left, right, (((1,), (1,)), ((), ())), preferred_element_type=F32)


def nn(left, right):
    return jnp.dot(left, right, preferred_element_type=F32)


def mod(value, size):
    return lax.rem(value + size, size)


def rows16(block):
    return pl.ds(pl.multiple_of(block * 16, 16), 16)


def unit_cols(unit):
    return pl.ds(pl.multiple_of(unit * UNIT, UNIT), UNIT)


def kernel(
    hid, og, w, adt, au,
    hg, rec, gd, gu,
    W, H, G, I, O, Ob, R1, R2, ADT, AU, PD, PU, DT, UT, GDs, GDr, GUs, GUr, OXn, OXf, OPs, OPr, LOW, LOWO,
    lsem, wds, wdr, wfs, wfr, hs, hr, gzs, gzr, gxs, gxr, pds, pdr, pus, pur, gys, gyr,
    r1s, r1r, r2s, r2r, oxs, oxr, ops_, opr,
):
    gx, gy, gz = lax.axis_index("gx"), lax.axis_index("gy"), lax.axis_index("gz")
    y, zh = lax.div(gz, 2), lax.rem(gz, 2)
    z = zh * 8 + gy
    zc, zm = lax.rem(z, 4), lax.div(z, 4)

    def zdev(step):
        where = mod(z + step, 16)
        return {"gy": lax.rem(where, 8), "gz": y * 2 + lax.div(where, 8)}

    def ydev(where):
        return {"gz": where * 2 + zh}

    def xdev(step):
        return {"gx": mod(gx + step, 8)}

    yup, ydown, yfar = mod(y + 1, 4), mod(y - 1, 4), mod(y + 2, 4)
    partner = {"gz": y * 2 + (1 - zh)}

    def remote(src, dst, ssem, rsem, to):
        return pltpu.make_async_remote_copy(
            src_ref=src, dst_ref=dst, send_sem=ssem, recv_sem=rsem, device_id=to, device_id_type=MESH
        )

    def got(part, sem):
        remote(part, part, sem, sem, xdev(1)).wait_recv()

    def left(part, sem):
        remote(part, part, sem, sem, xdev(1)).wait_send()

    def rows_of(where):
        return rows16(lax.rem(where, 4) * 4 + lax.div(where, 4))

    def quarter(q, which):
        return pl.ds(pl.multiple_of((2 * q + which) * 256, 256), 256)

    def cols_of(where):
        return pl.ds(pl.multiple_of(where * 256, 256), 256)

    my_cols = cols_of(y)
    mine = rows_of(zh * 8 + gx)
    theirs = rows_of((1 - zh) * 8 + gx)

    loads = [
        pltpu.make_async_copy(hid, H.at[rows_of(z), :], lsem.at[0]),
        pltpu.make_async_copy(w, W.at[:, my_cols], lsem.at[1]),
        pltpu.make_async_copy(adt, ADT, lsem.at[2]),
    ]
    for q in range(4):
        loads.append(pltpu.make_async_copy(og.at[:, quarter(q, zh)], G.at[mine, q * 256:(q + 1) * 256], lsem.at[3 + q]))
        loads.append(pltpu.make_async_copy(au.at[:, quarter(q, zh)], AU.at[:, q * 256:(q + 1) * 256], lsem.at[7 + q]))
    for load in loads:
        load.start()

    barrier = pltpu.get_barrier_semaphore()
    peers = [zdev(i) for i in (1, -1, 2, -2, 4, -4, 8)] + [ydev(yup), ydev(ydown), ydev(yfar)]
    peers += [xdev(i) for i in range(1, 8)]
    for peer in peers:
        pl.semaphore_signal(barrier, inc=1, device_id=peer, device_id_type=MESH)
    pl.semaphore_wait(barrier, len(peers))

    def w_rows(unit):
        return pl.ds(pl.multiple_of(unit * UNIT, UNIT), UNIT)

    def w_chunk(chunk):
        return pl.ds(pl.multiple_of(chunk * CHUNK, CHUNK), CHUNK)

    def w_half(chunk, side):
        return pl.ds(pl.multiple_of(chunk * CHUNK + side * HALF, HALF), HALF)

    def w_direct(unit, side):
        return remote(
            w.at[w_chunk(unit), :], W.at[w_chunk(unit), my_cols], wds.at[side], wdr.at[side, unit],
            ydev(yup if side == 0 else ydown),
        )

    def w_pass(unit, side):
        part = W.at[w_half(unit, side), cols_of(ydown if side == 0 else yup)]
        return remote(part, part, wfs.at[side], wfr.at[side, unit], ydev(yup if side == 0 else ydown))

    def w_step(unit):
        @pl.when(unit + AHEAD < CHUNKS)
        def _():
            w_direct(unit + AHEAD, 0).start()
            w_direct(unit + AHEAD, 1).start()

        for side in range(2):
            got(W.at[w_chunk(unit), cols_of(ydown if side == 0 else yup)], wdr.at[side, unit])
            w_pass(unit, side).start()

    for unit in range(AHEAD):
        w_direct(unit, 0).start()
        w_direct(unit, 1).start()

    for q in range(4):
        remote(og.at[:, quarter(q, 1 - zh)], G.at[mine, q * 256:(q + 1) * 256], gzs, gzr, partner).start()

    def h_move(step, side):
        part = H.at[rows_of(mod(z - step if side == 0 else z + step, 16)), :]
        return remote(part, part, hs.at[side], hr.at[side, step], zdev(1 if side == 0 else -1))

    def h_step(step):
        got(H.at[rows_of(mod(z - 1 - step, 16)), :], hr.at[0, step])

        @pl.when(step < 7)
        def _():
            h_move(step + 1, 0).start()
            got(H.at[rows_of(mod(z + 1 + step, 16)), :], hr.at[1, step])

        @pl.when(step < 6)
        def _():
            h_move(step + 1, 1).start()

    loads[0].wait()
    h_move(0, 0).start()
    h_move(0, 1).start()

    def g_send(i, rows, which):
        return remote(G.at[rows, :], G.at[rows, :], gxs.at[which], gxr.at[which], xdev(i))

    for load in loads[2:]:
        load.wait()
    for i in range(1, 8):
        g_send(i, mine, 0).start()
    O[...] = jnp.zeros_like(O)
    loads[1].wait()

    pd_steps = ((1, -1, 2), (4, -4, 8))

    def pd_send(stage, i):
        return remote(
            PD.at[stage, 0], PD.at[stage, i + 1], pds.at[stage, i], pdr.at[stage, i], zdev(pd_steps[stage][i])
        )

    def pd_sum(stage):
        for i in range(3):
            got(PD.at[stage, i + 1], pdr.at[stage, i])
        return sum(PD[stage, i].astype(F32) for i in range(4))

    def pu_send(i):
        return remote(PU.at[0], PU.at[i], pus, pur.at[i - 1], xdev(i))

    def up_unit(unit, total):
        return total + nt(ADT[:, unit_cols(unit)], H[:, unit_cols(unit)])

    def window(where):
        block = 2 * where + zh
        return pl.ds(pl.multiple_of(lax.div(block * 13, 4) * 128, 128), WIN)

    def gy_send(kind, i):
        src, dst = (GDs.at[i - 1], GDr.at[i - 1]) if kind == 0 else (GUs.at[i - 1], GUr.at[i - 1])
        return remote(src, dst, gys.at[kind, i - 1], gyr.at[kind, i - 1], ydev(mod(y + i, 4)))

    class_rows = pl.ds(pl.multiple_of(zc * 64, 64), 64)

    def r1_send(unit, i):
        step = (1, -1, 2 - 4 * lax.rem(unit, 2))[i]
        rows = pl.ds(pl.multiple_of(lax.rem(z + step + 16, 4) * 64, 64), 64)
        cols = unit_cols(unit)
        return remote(I.at[rows, cols], R1.at[i, :, cols], r1s.at[i], r1r.at[i, unit], zdev(step))

    def r2_send(unit, i):
        rows = rows16(lax.rem(zm + i + 1, 4))
        cols = unit_cols(unit)
        return remote(
            R1.at[0, rows, cols], R2.at[i, :, cols], r2s.at[i], r2r.at[i, unit], zdev((4, 8, -4)[i])
        )

    def input_unit(unit):
        for side in range(2):
            for chunk in (2 * unit, 2 * unit + 1):
                got(W.at[w_half(chunk, side), cols_of(yfar)], wfr.at[side, chunk])
        I[:, unit_cols(unit)] = nt(G[...], W[w_rows(unit), :]).astype(BF)
        for i in range(3):
            r1_send(unit, i).start()

    def input_class(unit):
        cols = unit_cols(unit)
        for i in range(3):
            got(R1.at[i, :, cols], r1r.at[i, unit])
        total = I[class_rows, cols].astype(F32)
        for i in range(3):
            total = total + R1[i, :, cols].astype(F32)
        R1[0, :, cols] = total.astype(BF)
        for i in range(3):
            r2_send(unit, i).start()

    def pick(where):
        first = (lax.rem(where, 4) * 4 + lax.div(where, 4)) * 16
        return (
            lax.broadcasted_iota(jnp.int32, (16, TOK), 1) == lax.broadcasted_iota(jnp.int32, (16, TOK), 0) + first
        ).astype(BF)

    def input_end(unit):
        cols = unit_cols(unit)
        for i in range(3):
            got(R2.at[i, :, cols], r2r.at[i, unit])
        total = R1[0, rows16(zm), cols].astype(F32)
        for i in range(3):
            total = total + R2[i, :, cols].astype(F32)
        hg[:, cols] = (total + LOW[:, cols]).astype(BF)

    order = (0, 1, 3, 2)

    def output_unit(places, unit):
        block = H[:, unit_cols(unit)]
        for q in places:
            O[:, q * 256:(q + 1) * 256] += nn(block, W[w_rows(unit), cols_of(mod(y + order[q], 4))])

    def ox_send(far, i, which):
        to = mod(gx + i, 8)
        rows = rows_of(which * 8 + to)
        src = Ob.at[rows, 768:1024] if far else Ob.at[rows, 0:768]
        return remote(src, (OXf if far else OXn).at[i, which], oxs.at[far], oxr.at[far], xdev(i))

    def ox_go(far):
        lo, hi = (768, 1024) if far else (0, 768)
        Ob[:, lo:hi] = O[:, lo:hi].astype(BF)
        for i in range(1, 8):
            for which in range(2):
                ox_send(far, i, which).start()

    def op_send(far):
        lo, hi = (768, 1024) if far else (0, 768)
        return remote(OPs.at[:, lo:hi], OPr.at[:, lo:hi], ops_.at[far], opr.at[far], partner)

    def ox_sum(far):
        lo, hi = (768, 1024) if far else (0, 768)
        OX = OXf if far else OXn
        got(OX.at[1:8], oxr.at[far])
        for which, half in ((0, 1 - zh), (1, zh)):
            total = O[rows_of(half * 8 + gx), lo:hi]
            for i in range(1, 8):
                total = total + OX[i, half].astype(F32)
            total = (total + LOWO[which, :, lo:hi]).astype(BF)
            for q in range(lo // 256, hi // 256):
                part = total[:, q * 256 - lo:(q + 1) * 256 - lo]
                if which == 0:
                    OPs[:, q * 256:(q + 1) * 256] = part
                else:
                    rec[:, quarter(mod(y + order[q], 4), zh)] = part
            if which == 0:
                op_send(far).start()

    def op_end(far):
        lo, hi = (768, 1024) if far else (0, 768)
        got(OPr.at[:, lo:hi], opr.at[far])
        for q in range(lo // 256, hi // 256):
            rec[:, quarter(mod(y + order[q], 4), 1 - zh)] = OPr[:, q * 256:(q + 1) * 256]

    def loop(j, _):
        w_step(2 * j)

        @pl.when((j >= H_LAG) & (j < 8 + H_LAG))
        def _():
            h_step(j - H_LAG)

        @pl.when(j == 1)
        def _():
            got(G.at[theirs, :], gzr)
            for i in range(1, 8):
                g_send(i, theirs, 1).start()

        w_step(2 * j + 1)

        @pl.when(j == 2)
        def _():
            for which in range(2):
                got(G.at[0:112, :], gxr.at[which])
            PD[0, 0] = nt(AU[...], G[...]).astype(BF)
            for i in range(3):
                pd_send(0, i).start()

        @pl.when(j >= 2)
        def _():
            input_unit(j - 2)

        first = lax.min(4 * (j - 9), UNITS - 1)
        last = lax.min(4 * (j - 8), UNITS)

        @pl.when(j >= 9)
        def _():
            def near(unit, _):
                output_unit((0, 1, 2), unit)
                return 0

            lax.fori_loop(first, last, near, 0)

        @pl.when(j == UNITS - 1)
        def _():
            ox_go(0)

        far_first = lax.min(4 * (j - 9), j - 2)
        far_last = lax.min(4 * (j - 8), j - 1)

        @pl.when(j >= 9)
        def _():
            def far(unit, _):
                output_unit((3,), unit)
                return 0

            lax.fori_loop(far_first, far_last, far, 0)

        @pl.when(j == 3)
        def _():
            PD[1, 0] = pd_sum(0).astype(BF)
            for i in range(3):
                pd_send(1, i).start()

        @pl.when(j == 4)
        def _():
            DT[...] = pd_sum(1).astype(BF)

        def classes(turn):
            late = (turn >= 10).astype(jnp.int32) + (turn >= 12).astype(jnp.int32)
            return lax.max(turn - 4 + late, 0)

        def class_body(unit, _):
            input_class(unit)
            return 0

        lax.fori_loop(classes(j - 1), classes(j), class_body, 0)

        @pl.when(j >= END_LAG)
        def _():
            input_end(j - END_LAG)

        @pl.when(j == 8 + H_LAG)
        def _():
            PU[0] = lax.fori_loop(0, UNITS, up_unit, jnp.zeros((16, TOK), F32))
            for i in range(1, 8):
                pu_send(i).start()
            for i in range(1, 4):
                GDs[i - 1] = nn(DT[...], H[:, window(mod(y + i, 4))]).astype(BF)

        @pl.when(j == 9 + H_LAG)
        def _():
            total = PU[0]
            for i in range(1, 8):
                got(PU.at[i], pur.at[i - 1])
                total = total + PU[i]
            UT[...] = total.astype(BF)
            for i in range(1, 4):
                GUs[i - 1] = nn(UT[...], G[:, cols_of(mod(y + i, 4))]).astype(BF)

        @pl.when(j == 5)
        def _():
            low = nt(pick(z), DT[...]).astype(BF)
            LOW[...] = 2.0 * nn(low, ADT[...])

        @pl.when(j == 10 + H_LAG)
        def _():
            for which, half in ((0, 1 - zh), (1, zh)):
                low = nt(pick(half * 8 + gx), UT[...]).astype(BF)
                for q in range(4):
                    LOWO[which, :, q * 256:(q + 1) * 256] = 2.0 * nn(low, AU[:, cols_of(mod(y + order[q], 4))])

        return 0

    lax.fori_loop(0, UNITS, loop, 0)

    def over(first, last, work):
        def body(unit, _):
            work(unit)
            return 0

        lax.fori_loop(first, last, body, 0)

    def last_unit(unit):
        input_unit(unit)
        output_unit((3,), unit)

    for i in range(1, 4):
        gy_send(0, i).start()
        gy_send(1, i).start()
    over(UNITS - 2, UNITS, last_unit)
    ox_go(1)
    over(UNITS - CLASS_LEFT, UNITS - 1, input_class)
    ox_sum(0)
    over(UNITS - 1, UNITS, input_class)
    ox_sum(1)
    over(UNITS - END_LAG, UNITS - 1, input_end)
    total_down = nn(DT[...], H[:, window(y)])
    total_up = nn(UT[...], G[:, my_cols])
    for i in range(1, 4):
        got(GDr.at[i - 1], gyr.at[0, i - 1])
        got(GUr.at[i - 1], gyr.at[1, i - 1])
        total_down = total_down + GDr[i - 1].astype(F32)
        total_up = total_up + GUr[i - 1].astype(F32)
    gd[...] = total_down * (2.0 / 1024)
    gu[...] = total_up * (2.0 / 1024)

    left(G.at[mine, :], gzs)
    for which in range(2):
        left(G.at[0:112, :], gxs.at[which])
    left(PU.at[1:8], pus)
    for i in range(3):
        for stage in range(2):
            pd_send(stage, i).wait_send()
            gy_send(stage, i + 1).wait_send()
        left(I.at[0:64, :], r1s.at[i])
        left(I.at[0:16, :], r2s.at[i])
    left(H.at[0:128, :], hs.at[0])
    left(H.at[0:112, :], hs.at[1])
    for side in range(2):
        left(W.at[:, 0:256], wds.at[side])
        left(W.at[0:FF // 2, 0:256], wfs.at[side])
    left(OXn.at[1:8], oxs.at[0])
    left(OXf.at[1:8], oxs.at[1])
    over(UNITS - 1, UNITS, input_end)
    for far in range(2):
        op_end(far)
        op_send(far).wait_send()


def hand_over(hg_in, rec_in, gd_in, gu_in, hg, rec, gd, gu):
    hg[...] = hg_in[...]
    rec[...] = rec_in[...]
    gu[...] = gu_in[...]
    place = lax.rem(lax.axis_index("gz"), 4)
    for k in range(4):
        @pl.when(place == k)
        def _(k=k):
            gd[...] = gd_in[:, 32 * k:32 * k + FF // 8]


def shards(hidden, out_grad, weight, adapter_down_factor, adapter_up_factor):
    any_spec = pl.BlockSpec(memory_space=pl.ANY)
    vmem_spec = pl.BlockSpec(memory_space=pltpu.VMEM)
    dma = pltpu.SemaphoreType.DMA
    hg, rec, gd, gu = pl.pallas_call(
        kernel,
        out_shape=(
            jax.ShapeDtypeStruct((16, FF), BF),
            jax.ShapeDtypeStruct((16, 2048), BF),
            jax.ShapeDtypeStruct((16, WIN), F32),
            jax.ShapeDtypeStruct((16, 256), F32),
        ),
        in_specs=[any_spec] * 5,
        out_specs=(vmem_spec,) * 4,
        scratch_shapes=[
            pltpu.VMEM((FF, FEAT), BF),
            pltpu.VMEM((TOK, FF), BF),
            pltpu.VMEM((TOK, FEAT), BF),
            pltpu.VMEM((TOK, FF), BF),
            pltpu.VMEM((TOK, FEAT), F32),
            pltpu.VMEM((TOK, FEAT), BF),
            pltpu.VMEM((3, 64, FF), BF),
            pltpu.VMEM((3, 16, FF), BF),
            pltpu.VMEM((16, FF), BF),
            pltpu.VMEM((16, FEAT), BF),
            pltpu.VMEM((2, 4, 16, TOK), BF),
            pltpu.VMEM((8, 16, TOK), F32),
            pltpu.VMEM((16, TOK), BF),
            pltpu.VMEM((16, TOK), BF),
            pltpu.VMEM((3, 16, WIN), BF),
            pltpu.VMEM((3, 16, WIN), BF),
            pltpu.VMEM((3, 16, 256), BF),
            pltpu.VMEM((3, 16, 256), BF),
            pltpu.VMEM((8, 2, 16, 768), BF),
            pltpu.VMEM((8, 2, 16, 256), BF),
            pltpu.VMEM((16, FEAT), BF),
            pltpu.VMEM((16, FEAT), BF),
            pltpu.VMEM((16, FF), F32),
            pltpu.VMEM((2, 16, FEAT), F32),
            dma((11,)),
            dma((2,)), dma((2, CHUNKS)),
            dma((2,)), dma((2, CHUNKS)),
            dma((2,)), dma((2, 8)),
            dma, dma,
            dma((2,)), dma((2,)),
            dma((2, 3)), dma((2, 3)),
            dma, dma((7,)),
            dma((2, 3)), dma((2, 3)),
            dma((3,)), dma((3, UNITS)),
            dma((3,)), dma((3, UNITS)),
            dma((2,)), dma((2,)),
            dma((2,)), dma((2,)),
        ],
        compiler_params=pltpu.CompilerParams(
            collective_id=0, has_side_effects=True, vmem_limit_bytes=63 * 1024 * 1024
        ),
    )(hidden, out_grad, weight, adapter_down_factor.T, adapter_up_factor)
    hg, rec, gd, gu = pl.pallas_call(
        hand_over,
        out_shape=(
            jax.ShapeDtypeStruct((16, FF), BF),
            jax.ShapeDtypeStruct((16, 2048), BF),
            jax.ShapeDtypeStruct((16, FF // 8), F32),
            jax.ShapeDtypeStruct((16, 256), F32),
        ),
        in_specs=[vmem_spec] * 4,
        out_specs=(vmem_spec,) * 4,
    )(hg, rec, gd, gu)
    return hg, rec, gd.T, gu


def solution(mesh):
    placed = (
        P(("gz", "gy"), "gx"),
        P(("gz", "gx"), "gy"),
        P("gx", ("gy", "gz")),
        P("gx", None),
        P(None, "gy"),
    )
    return jax.shard_map(
        shards,
        mesh=mesh,
        in_specs=placed,
        out_specs=(
            P(("gz", "gy"), "gx"),
            P(("gz", "gx"), "gy"),
            P(("gx", "gz"), None),
            P(None, ("gy", "gz")),
        ),
        check_vma=False,
    )
```

```python
import functools

import jax
import jax.numpy as jnp
from jax import lax
from jax.experimental import pallas as pl
from jax.experimental.pallas import tpu as pltpu
from jax.sharding import PartitionSpec as P

MESH = pl.DeviceIdType.MESH
BF = jnp.bfloat16
F32 = jnp.float32

FF = 3328
UNIT = 256
UNITS = FF // UNIT
CHUNK = 64
CHUNKS = FF // CHUNK
HALF = CHUNK // 2
TOK = 256
FEAT = 1024
AHEAD = 10
CLASS_LEFT = 3
END_LAG = 8
H_LAG = 1
WIN = 512


def nt(left, right):
    return lax.dot_general(left, right, (((1,), (1,)), ((), ())), preferred_element_type=F32)


def nn(left, right):
    return jnp.dot(left, right, preferred_element_type=F32)


def mod(value, size):
    return lax.rem(value + size, size)


def rows16(block):
    return pl.ds(pl.multiple_of(block * 16, 16), 16)


def unit_cols(unit):
    return pl.ds(pl.multiple_of(unit * UNIT, UNIT), UNIT)


def kernel(
    hid, og, w, adt, au,
    hg, rec, gd, gu,
    W, H, G, I, O, Ob, R1, R2, ADT, AU, PD, PU, DT, UT, GDs, GDr, GUs, GUr, OXn, OXf, OPs, OPr, LOW, LOWO,
    lsem, wds, wdr, wfs, wfr, hs, hr, gzs, gzr, gxs, gxr, pds, pdr, pus, pur, gys, gyr,
    r1s, r1r, r2s, r2r, oxs, oxr, ops_, opr,
):
    gx, gy, gz = lax.axis_index("gx"), lax.axis_index("gy"), lax.axis_index("gz")
    y, zh = lax.div(gz, 2), lax.rem(gz, 2)
    z = zh * 8 + gy
    zc, zm = lax.rem(z, 4), lax.div(z, 4)

    def zdev(step):
        where = mod(z + step, 16)
        return {"gy": lax.rem(where, 8), "gz": y * 2 + lax.div(where, 8)}

    def ydev(where):
        return {"gz": where * 2 + zh}

    def xdev(step):
        return {"gx": mod(gx + step, 8)}

    yup, ydown, yfar = mod(y + 1, 4), mod(y - 1, 4), mod(y + 2, 4)
    partner = {"gz": y * 2 + (1 - zh)}

    def remote(src, dst, ssem, rsem, to):
        return pltpu.make_async_remote_copy(
            src_ref=src, dst_ref=dst, send_sem=ssem, recv_sem=rsem, device_id=to, device_id_type=MESH
        )

    def got(part, sem):
        remote(part, part, sem, sem, xdev(1)).wait_recv()

    def left(part, sem):
        remote(part, part, sem, sem, xdev(1)).wait_send()

    def rows_of(where):
        return rows16(lax.rem(where, 4) * 4 + lax.div(where, 4))

    def quarter(q, which):
        return pl.ds(pl.multiple_of((2 * q + which) * 256, 256), 256)

    def cols_of(where):
        return pl.ds(pl.multiple_of(where * 256, 256), 256)

    my_cols = cols_of(y)
    mine = rows_of(zh * 8 + gx)
    theirs = rows_of((1 - zh) * 8 + gx)

    loads = [
        pltpu.make_async_copy(hid, H.at[rows_of(z), :], lsem.at[0]),
        pltpu.make_async_copy(w, W.at[:, my_cols], lsem.at[1]),
        pltpu.make_async_copy(adt, ADT, lsem.at[2]),
    ]
    for q in range(4):
        loads.append(pltpu.make_async_copy(og.at[:, quarter(q, zh)], G.at[mine, q * 256:(q + 1) * 256], lsem.at[3 + q]))
        loads.append(pltpu.make_async_copy(au.at[:, quarter(q, zh)], AU.at[:, q * 256:(q + 1) * 256], lsem.at[7 + q]))
    for load in loads:
        load.start()

    barrier = pltpu.get_barrier_semaphore()
    peers = [zdev(i) for i in (1, -1, 2, -2, 4, -4, 8)] + [ydev(yup), ydev(ydown), ydev(yfar)]
    peers += [xdev(i) for i in range(1, 8)]
    for peer in peers:
        pl.semaphore_signal(barrier, inc=1, device_id=peer, device_id_type=MESH)
    pl.semaphore_wait(barrier, len(peers))

    def w_rows(unit):
        return pl.ds(pl.multiple_of(unit * UNIT, UNIT), UNIT)

    def w_chunk(chunk):
        return pl.ds(pl.multiple_of(chunk * CHUNK, CHUNK), CHUNK)

    def w_half(chunk, side):
        return pl.ds(pl.multiple_of(chunk * CHUNK + side * HALF, HALF), HALF)

    def w_direct(unit, side):
        return remote(
            w.at[w_chunk(unit), :], W.at[w_chunk(unit), my_cols], wds.at[side], wdr.at[side, unit],
            ydev(yup if side == 0 else ydown),
        )

    def w_pass(unit, side):
        part = W.at[w_half(unit, side), cols_of(ydown if side == 0 else yup)]
        return remote(part, part, wfs.at[side], wfr.at[side, unit], ydev(yup if side == 0 else ydown))

    def w_step(unit):
        @pl.when(unit + AHEAD < CHUNKS)
        def _():
            w_direct(unit + AHEAD, 0).start()
            w_direct(unit + AHEAD, 1).start()

        for side in range(2):
            got(W.at[w_chunk(unit), cols_of(ydown if side == 0 else yup)], wdr.at[side, unit])
            w_pass(unit, side).start()

    for unit in range(AHEAD):
        w_direct(unit, 0).start()
        w_direct(unit, 1).start()

    for q in range(4):
        remote(og.at[:, quarter(q, 1 - zh)], G.at[mine, q * 256:(q + 1) * 256], gzs, gzr, partner).start()

    def h_move(step, side):
        part = H.at[rows_of(mod(z - step if side == 0 else z + step, 16)), :]
        return remote(part, part, hs.at[side], hr.at[side, step], zdev(1 if side == 0 else -1))

    def h_step(step):
        got(H.at[rows_of(mod(z - 1 - step, 16)), :], hr.at[0, step])

        @pl.when(step < 7)
        def _():
            h_move(step + 1, 0).start()
            got(H.at[rows_of(mod(z + 1 + step, 16)), :], hr.at[1, step])

        @pl.when(step < 6)
        def _():
            h_move(step + 1, 1).start()

    loads[0].wait()
    h_move(0, 0).start()
    h_move(0, 1).start()

    def g_send(i, rows, which):
        return remote(G.at[rows, :], G.at[rows, :], gxs.at[which], gxr.at[which], xdev(i))

    for load in loads[2:]:
        load.wait()
    for i in range(1, 8):
        g_send(i, mine, 0).start()
    O[...] = jnp.zeros_like(O)
    loads[1].wait()

    pd_steps = ((1, -1, 2), (4, -4, 8))

    def pd_send(stage, i):
        return remote(
            PD.at[stage, 0], PD.at[stage, i + 1], pds.at[stage, i], pdr.at[stage, i], zdev(pd_steps[stage][i])
        )

    def pd_sum(stage):
        for i in range(3):
            got(PD.at[stage, i + 1], pdr.at[stage, i])
        return sum(PD[stage, i].astype(F32) for i in range(4))

    def pu_send(i):
        return remote(PU.at[0], PU.at[i], pus, pur.at[i - 1], xdev(i))

    def up_unit(unit, total):
        return total + nt(ADT[:, unit_cols(unit)], H[:, unit_cols(unit)])

    def window(where):
        block = 2 * where + zh
        return pl.ds(pl.multiple_of(lax.div(block * 13, 4) * 128, 128), WIN)

    def gy_send(kind, i):
        src, dst = (GDs.at[i - 1], GDr.at[i - 1]) if kind == 0 else (GUs.at[i - 1], GUr.at[i - 1])
        return remote(src, dst, gys.at[kind, i - 1], gyr.at[kind, i - 1], ydev(mod(y + i, 4)))

    class_rows = pl.ds(pl.multiple_of(zc * 64, 64), 64)

    def r1_send(unit, i):
        step = (1, -1, 2 - 4 * lax.rem(unit, 2))[i]
        rows = pl.ds(pl.multiple_of(lax.rem(z + step + 16, 4) * 64, 64), 64)
        cols = unit_cols(unit)
        return remote(I.at[rows, cols], R1.at[i, :, cols], r1s.at[i], r1r.at[i, unit], zdev(step))

    def r2_send(unit, i):
        rows = rows16(lax.rem(zm + i + 1, 4))
        cols = unit_cols(unit)
        return remote(
            R1.at[0, rows, cols], R2.at[i, :, cols], r2s.at[i], r2r.at[i, unit], zdev((4, 8, -4)[i])
        )

    def input_unit(unit):
        for side in range(2):
            for part in range(4):
                chunk = 4 * unit + part
                got(W.at[w_half(chunk, side), cols_of(yfar)], wfr.at[side, chunk])
        I[:, unit_cols(unit)] = nt(G[...], W[w_rows(unit), :]).astype(BF)
        for i in range(3):
            r1_send(unit, i).start()

    def input_class(unit):
        cols = unit_cols(unit)
        for i in range(3):
            got(R1.at[i, :, cols], r1r.at[i, unit])
        total = I[class_rows, cols].astype(F32)
        for i in range(3):
            total = total + R1[i, :, cols].astype(F32)
        R1[0, :, cols] = total.astype(BF)
        for i in range(3):
            r2_send(unit, i).start()

    def pick(where):
        first = (lax.rem(where, 4) * 4 + lax.div(where, 4)) * 16
        return (
            lax.broadcasted_iota(jnp.int32, (16, TOK), 1) == lax.broadcasted_iota(jnp.int32, (16, TOK), 0) + first
        ).astype(BF)

    def input_end(unit):
        cols = unit_cols(unit)
        for i in range(3):
            got(R2.at[i, :, cols], r2r.at[i, unit])
        total = R1[0, rows16(zm), cols].astype(F32)
        for i in range(3):
            total = total + R2[i, :, cols].astype(F32)
        hg[:, cols] = (total + LOW[:, cols]).astype(BF)

    order = (0, 1, 3, 2)

    def output_unit(places, unit):
        block = H[:, unit_cols(unit)]
        for q in places:
            O[:, q * 256:(q + 1) * 256] += nn(block, W[w_rows(unit), cols_of(mod(y + order[q], 4))])

    def ox_send(far, i, which):
        to = mod(gx + i, 8)
        rows = rows_of(which * 8 + to)
        src = Ob.at[rows, 768:1024] if far else Ob.at[rows, 0:768]
        return remote(src, (OXf if far else OXn).at[i, which], oxs.at[far], oxr.at[far], xdev(i))

    def ox_go(far):
        lo, hi = (768, 1024) if far else (0, 768)
        Ob[:, lo:hi] = O[:, lo:hi].astype(BF)
        for i in range(1, 8):
            for which in range(2):
                ox_send(far, i, which).start()

    def op_send(far):
        lo, hi = (768, 1024) if far else (0, 768)
        return remote(OPs.at[:, lo:hi], OPr.at[:, lo:hi], ops_.at[far], opr.at[far], partner)

    def ox_sum(far):
        lo, hi = (768, 1024) if far else (0, 768)
        OX = OXf if far else OXn
        got(OX.at[1:8], oxr.at[far])
        for which, half in ((0, 1 - zh), (1, zh)):
            total = O[rows_of(half * 8 + gx), lo:hi]
            for i in range(1, 8):
                total = total + OX[i, half].astype(F32)
            total = (total + LOWO[which, :, lo:hi]).astype(BF)
            for q in range(lo // 256, hi // 256):
                part = total[:, q * 256 - lo:(q + 1) * 256 - lo]
                if which == 0:
                    OPs[:, q * 256:(q + 1) * 256] = part
                else:
                    rec[:, quarter(mod(y + order[q], 4), zh)] = part
            if which == 0:
                op_send(far).start()

    def op_end(far):
        lo, hi = (768, 1024) if far else (0, 768)
        got(OPr.at[:, lo:hi], opr.at[far])
        for q in range(lo // 256, hi // 256):
            rec[:, quarter(mod(y + order[q], 4), 1 - zh)] = OPr[:, q * 256:(q + 1) * 256]

    def loop(j, _):
        w_step(4 * j)
        w_step(4 * j + 1)

        @pl.when((j >= H_LAG) & (j < 8 + H_LAG))
        def _():
            h_step(j - H_LAG)

        @pl.when(j == 1)
        def _():
            got(G.at[theirs, :], gzr)
            for i in range(1, 8):
                g_send(i, theirs, 1).start()

        w_step(4 * j + 2)
        w_step(4 * j + 3)

        @pl.when(j == 2)
        def _():
            for which in range(2):
                got(G.at[0:112, :], gxr.at[which])
            PD[0, 0] = nt(AU[...], G[...]).astype(BF)
            for i in range(3):
                pd_send(0, i).start()

        @pl.when(j >= 2)
        def _():
            input_unit(j - 2)

        first = lax.min(4 * (j - 9), UNITS - 1)
        last = lax.min(4 * (j - 8), UNITS)

        @pl.when(j >= 9)
        def _():
            def near(unit, _):
                output_unit((0, 1, 2), unit)
                return 0

            lax.fori_loop(first, last, near, 0)

        @pl.when(j == UNITS - 1)
        def _():
            ox_go(0)

        far_first = lax.min(4 * (j - 9), j - 2)
        far_last = lax.min(4 * (j - 8), j - 1)

        @pl.when(j >= 9)
        def _():
            def far(unit, _):
                output_unit((3,), unit)
                return 0

            lax.fori_loop(far_first, far_last, far, 0)

        @pl.when(j == 3)
        def _():
            PD[1, 0] = pd_sum(0).astype(BF)
            for i in range(3):
                pd_send(1, i).start()

        @pl.when(j == 4)
        def _():
            DT[...] = pd_sum(1).astype(BF)

        def classes(turn):
            late = (turn >= 10).astype(jnp.int32) + (turn >= 12).astype(jnp.int32)
            return lax.max(turn - 4 + late, 0)

        def class_body(unit, _):
            input_class(unit)
            return 0

        lax.fori_loop(classes(j - 1), classes(j), class_body, 0)

        @pl.when(j >= END_LAG)
        def _():
            input_end(j - END_LAG)

        @pl.when(j == 8 + H_LAG)
        def _():
            PU[0] = lax.fori_loop(0, UNITS, up_unit, jnp.zeros((16, TOK), F32))
            for i in range(1, 8):
                pu_send(i).start()
            for i in range(1, 4):
                GDs[i - 1] = nn(DT[...], H[:, window(mod(y + i, 4))]).astype(BF)

        @pl.when(j == 9 + H_LAG)
        def _():
            total = PU[0]
            for i in range(1, 8):
                got(PU.at[i], pur.at[i - 1])
                total = total + PU[i]
            UT[...] = total.astype(BF)
            for i in range(1, 4):
                GUs[i - 1] = nn(UT[...], G[:, cols_of(mod(y + i, 4))]).astype(BF)

        @pl.when(j == 5)
        def _():
            low = nt(pick(z), DT[...]).astype(BF)
            LOW[...] = 2.0 * nn(low, ADT[...])

        @pl.when(j == 10 + H_LAG)
        def _():
            for which, half in ((0, 1 - zh), (1, zh)):
                low = nt(pick(half * 8 + gx), UT[...]).astype(BF)
                for q in range(4):
                    LOWO[which, :, q * 256:(q + 1) * 256] = 2.0 * nn(low, AU[:, cols_of(mod(y + order[q], 4))])

        return 0

    lax.fori_loop(0, UNITS, loop, 0)

    def over(first, last, work):
        def body(unit, _):
            work(unit)
            return 0

        lax.fori_loop(first, last, body, 0)

    def last_unit(unit):
        input_unit(unit)
        output_unit((3,), unit)

    for i in range(1, 4):
        gy_send(0, i).start()
        gy_send(1, i).start()
    over(UNITS - 2, UNITS, last_unit)
    ox_go(1)
    over(UNITS - CLASS_LEFT, UNITS - 1, input_class)
    ox_sum(0)
    over(UNITS - 1, UNITS, input_class)
    ox_sum(1)
    over(UNITS - END_LAG, UNITS - 1, input_end)
    total_down = nn(DT[...], H[:, window(y)])
    total_up = nn(UT[...], G[:, my_cols])
    for i in range(1, 4):
        got(GDr.at[i - 1], gyr.at[0, i - 1])
        got(GUr.at[i - 1], gyr.at[1, i - 1])
        total_down = total_down + GDr[i - 1].astype(F32)
        total_up = total_up + GUr[i - 1].astype(F32)
    gd[...] = total_down * (2.0 / 1024)
    gu[...] = total_up * (2.0 / 1024)

    left(G.at[mine, :], gzs)
    for which in range(2):
        left(G.at[0:112, :], gxs.at[which])
    left(PU.at[1:8], pus)
    for i in range(3):
        for stage in range(2):
            pd_send(stage, i).wait_send()
            gy_send(stage, i + 1).wait_send()
        left(I.at[0:64, :], r1s.at[i])
        left(I.at[0:16, :], r2s.at[i])
    left(H.at[0:128, :], hs.at[0])
    left(H.at[0:112, :], hs.at[1])
    for side in range(2):
        left(W.at[:, 0:256], wds.at[side])
        left(W.at[0:FF // 2, 0:256], wfs.at[side])
    left(OXn.at[1:8], oxs.at[0])
    left(OXf.at[1:8], oxs.at[1])
    over(UNITS - 1, UNITS, input_end)
    for far in range(2):
        op_end(far)
        op_send(far).wait_send()


def hand_over(hg_in, rec_in, gd_in, gu_in, hg, rec, gd, gu):
    hg[...] = hg_in[...]
    rec[...] = rec_in[...]
    gu[...] = gu_in[...]
    place = lax.rem(lax.axis_index("gz"), 4)
    for k in range(4):
        @pl.when(place == k)
        def _(k=k):
            gd[...] = gd_in[:, 32 * k:32 * k + FF // 8]


def shards(hidden, out_grad, weight, adapter_down_factor, adapter_up_factor):
    any_spec = pl.BlockSpec(memory_space=pl.ANY)
    vmem_spec = pl.BlockSpec(memory_space=pltpu.VMEM)
    dma = pltpu.SemaphoreType.DMA
    hg, rec, gd, gu = pl.pallas_call(
        kernel,
        out_shape=(
            jax.ShapeDtypeStruct((16, FF), BF),
            jax.ShapeDtypeStruct((16, 2048), BF),
            jax.ShapeDtypeStruct((16, WIN), F32),
            jax.ShapeDtypeStruct((16, 256), F32),
        ),
        in_specs=[any_spec] * 5,
        out_specs=(vmem_spec,) * 4,
        scratch_shapes=[
            pltpu.VMEM((FF, FEAT), BF),
            pltpu.VMEM((TOK, FF), BF),
            pltpu.VMEM((TOK, FEAT), BF),
            pltpu.VMEM((TOK, FF), BF),
            pltpu.VMEM((TOK, FEAT), F32),
            pltpu.VMEM((TOK, FEAT), BF),
            pltpu.VMEM((3, 64, FF), BF),
            pltpu.VMEM((3, 16, FF), BF),
            pltpu.VMEM((16, FF), BF),
            pltpu.VMEM((16, FEAT), BF),
            pltpu.VMEM((2, 4, 16, TOK), BF),
            pltpu.VMEM((8, 16, TOK), F32),
            pltpu.VMEM((16, TOK), BF),
            pltpu.VMEM((16, TOK), BF),
            pltpu.VMEM((3, 16, WIN), BF),
            pltpu.VMEM((3, 16, WIN), BF),
            pltpu.VMEM((3, 16, 256), BF),
            pltpu.VMEM((3, 16, 256), BF),
            pltpu.VMEM((8, 2, 16, 768), BF),
            pltpu.VMEM((8, 2, 16, 256), BF),
            pltpu.VMEM((16, FEAT), BF),
            pltpu.VMEM((16, FEAT), BF),
            pltpu.VMEM((16, FF), F32),
            pltpu.VMEM((2, 16, FEAT), F32),
            dma((11,)),
            dma((2,)), dma((2, CHUNKS)),
            dma((2,)), dma((2, CHUNKS)),
            dma((2,)), dma((2, 8)),
            dma, dma,
            dma((2,)), dma((2,)),
            dma((2, 3)), dma((2, 3)),
            dma, dma((7,)),
            dma((2, 3)), dma((2, 3)),
            dma((3,)), dma((3, UNITS)),
            dma((3,)), dma((3, UNITS)),
            dma((2,)), dma((2,)),
            dma((2,)), dma((2,)),
        ],
        compiler_params=pltpu.CompilerParams(
            collective_id=0, has_side_effects=True, vmem_limit_bytes=63 * 1024 * 1024
        ),
    )(hidden, out_grad, weight, adapter_down_factor.T, adapter_up_factor)
    hg, rec, gd, gu = pl.pallas_call(
        hand_over,
        out_shape=(
            jax.ShapeDtypeStruct((16, FF), BF),
            jax.ShapeDtypeStruct((16, 2048), BF),
            jax.ShapeDtypeStruct((16, FF // 8), F32),
            jax.ShapeDtypeStruct((16, 256), F32),
        ),
        in_specs=[vmem_spec] * 4,
        out_specs=(vmem_spec,) * 4,
    )(hg, rec, gd, gu)
    return hg, rec, gd.T, gu


def solution(mesh):
    placed = (
        P(("gz", "gy"), "gx"),
        P(("gz", "gx"), "gy"),
        P("gx", ("gy", "gz")),
        P("gx", None),
        P(None, "gy"),
    )
    return jax.shard_map(
        shards,
        mesh=mesh,
        in_specs=placed,
        out_specs=(
            P(("gz", "gy"), "gx"),
            P(("gz", "gx"), "gy"),
            P(("gx", "gz"), None),
            P(None, ("gy", "gz")),
        ),
        check_vma=False,
    )
```
